32 devices in a mesh: lat: 4 (over y, x), lon: 8 (over z, core).
Axes of the slice: x: 2, y: 2, z: 4, core: 2. Of those that a mesh axis runs over, the one named last changes fastest.
Arguments:
- state: bfloat16 [512, 1024, 128], P('lat', 'lon'), may hold values from -6 to 6
- edge_metric: float32 [9, 512, 1024], P(None, 'lat', 'lon'), may hold values from 0.1 to 1
- stencil_coef: float32 [2, 9, 128], replicated, may hold values from -4 to 4
- norm_gain: float32 [2, 128], replicated, may hold values from 0.25 to 1.75
- biases: float32 [2, 4, 128], replicated, may hold values from -3 to 3
- weights: bfloat16 [2, 896, 128], P(None, ('lat', 'lon')), may hold values from -0.5 to 0.5
Outputs:
- refined: bfloat16 [512, 1024, 128], P('lat', 'lon')
The draws below stay inside these ranges and needn't reach their ends.
All inputs are finite; a program needn't handle non-finite values.
Results may differ from the reference program's by a relative error of at most 0.0069.
Values may be sent and summed in bfloat16 or wider, within the bound.
No kernel may reach another device: no remote copies, remote signals or barrier semaphores. Data moves between devices by JAX's collectives and lax.ppermute only.
A program may use at most 128 MiB of HBM per device.

```python
import math
import jax
import jax.numpy as jnp
from jax import lax

C = 128
KMAT = 7
ITERS = 2
CLAT = 128
NLAT = 512
NLON = 1024
N_LAT = 4


def shard_levels(stream_key, extent, pieces, low, largest):
    def one(position, parts):
        draws = jax.random.uniform(jax.random.fold_in(jax.random.fold_in(stream_key, 6), position), (parts,), jnp.float32, low / len(pieces), largest / len(pieces))
        return jnp.repeat(jnp.exp(draws), extent[position] // parts).reshape((-1,) + (1,) * (len(extent) - position - 1))

    factor_of = one(*pieces[0])
    for cut in pieces[1:]:
        factor_of = factor_of * one(*cut)
    return factor_of


def gaussian(stream_key, shape, deviation, bound, cuts=(), held_as=jnp.bfloat16):
    entries = deviation * jax.random.normal(stream_key, shape, jnp.float32)
    if cuts:
        entries = entries * shard_levels(stream_key, shape, cuts, -0.22, 0.18)
    return jnp.clip(entries, -bound, bound).astype(held_as)


def setup_inputs(seed: int = 0) -> dict:
    seeds = jax.random.split(jax.random.key(seed), 7)
    return {
        "state": gaussian(seeds[0], (NLAT, NLON, C), 1.0, 6.0, ((0, 4), (1, 8))),
        "edge_metric": jnp.clip(jnp.exp(math.log(1.0) - 2.3025851 * jax.random.uniform(seeds[1], (9, NLAT, NLON), jnp.float32) ** shard_levels(seeds[1], (9, NLAT, NLON), ((1, 4), (2, 8)), -0.2, 0.2)), 0.1, 1.0),
        "stencil_coef": gaussian(seeds[2], (ITERS, 9, C), 1.0, 4.0, (), jnp.float32),
        "norm_gain": jnp.clip(1.0 + 0.15 * jax.random.normal(seeds[3], (ITERS, C), jnp.float32), 0.25, 1.75),
        "biases": gaussian(seeds[4], (ITERS, 4, C), 0.5, 3.0, (), jnp.float32),
        "weights": gaussian(seeds[5], (ITERS, KMAT * C, C), C ** -0.5, 0.5, ((1, 32),)),
    }


EPSILON = 1e-05

def grid_update(padded_rows, metric_rows, state_rows, coef, gain, bias, mats):
    row_count = state_rows.shape[0]
    col_count = state_rows.shape[1]
    channels = state_rows.shape[2]
    summed = jnp.zeros(state_rows.shape, jnp.float32)
    for lat_step in range(3):
        for lon_step in range(3):
            direction = 3 * lat_step + lon_step
            view = padded_rows[lat_step:lat_step + row_count, lon_step:lon_step + col_count].astype(jnp.float32)
            summed = summed + metric_rows[direction][:, :, None] * coef[direction] * view
    scale = lax.rsqrt(lax.optimization_barrier(jnp.mean(summed * summed, axis=-1, keepdims=True)) + EPSILON)
    normed = (summed * scale * gain).astype(jnp.bfloat16).reshape(-1, channels)
    hidden = state_rows.reshape(-1, channels)
    message = (jnp.dot(normed, mats[0], preferred_element_type=jnp.float32) + bias[0]).astype(jnp.bfloat16)
    update = jax.nn.sigmoid(jnp.dot(message, mats[1], preferred_element_type=jnp.float32) + jnp.dot(hidden, mats[4], preferred_element_type=jnp.float32) + bias[1])
    reset = jax.nn.sigmoid(jnp.dot(message, mats[2], preferred_element_type=jnp.float32) + jnp.dot(hidden, mats[5], preferred_element_type=jnp.float32) + bias[2])
    candidate = jnp.tanh(jnp.dot(message, mats[3], preferred_element_type=jnp.float32) + bias[3] + reset * jnp.dot(hidden, mats[6], preferred_element_type=jnp.float32))
    result = (1.0 - update) * candidate + update * hidden.astype(jnp.float32)
    return result.astype(jnp.bfloat16).reshape(state_rows.shape)

def pad_grid(current):
    half_cols = current.shape[1] // 2
    mirror = jnp.roll(jnp.stack([current[0], current[-1]]), -half_cols, axis=1)
    tall = jnp.concatenate([mirror[0:1], current, mirror[1:2]], axis=0)
    return jnp.concatenate([tall[:, -1:], tall, tall[:, :1]], axis=1)

def reference(state, edge_metric, stencil_coef, norm_gain, biases, weights):
    current = state
    for iteration in range(ITERS):
        padded = pad_grid(current)
        mats = weights[iteration].reshape(KMAT, C, C)
        coef = stencil_coef[iteration]
        gain = norm_gain[iteration]
        bias = biases[iteration]
        previous = current

        def one_block(block_index, padded=padded, previous=previous, mats=mats, coef=coef, gain=gain, bias=bias):
            start = (block_index * CLAT).astype(jnp.int32)
            rows_pad = lax.dynamic_slice_in_dim(padded, start, CLAT + 2, 0)
            rows_metric = lax.dynamic_slice_in_dim(edge_metric, start, CLAT, 1)
            rows_state = lax.dynamic_slice_in_dim(previous, start, CLAT, 0)
            return grid_update(rows_pad, rows_metric, rows_state, coef, gain, bias, mats)
        blocks = lax.map(one_block, jnp.arange(N_LAT, dtype=jnp.int32))
        current = blocks.reshape(previous.shape)
    return current
```

```python
import functools

import jax
import jax.numpy as jnp
from jax import lax
from jax.experimental import pallas as pl
from jax.experimental.pallas import tpu as pltpu
from jax.sharding import PartitionSpec as P

KMAT = 7
ITERS = 2
EPSILON = 1e-05
LANES = 128
BLOCK = 4
DEPTH = 4 * BLOCK
LINE = 136
F32 = jnp.float32
BF16 = jnp.bfloat16


def twice(a):
    return jnp.concatenate([a, a], axis=1)


def load_vectors(it, coef_ref, gain_ref, bias_ref, rows_s, coef_s, vec_s):
    rows_s[...] = jnp.zeros_like(rows_s)
    rows_s[0:9, :] = coef_ref[it]
    rows_s[9:10, :] = gain_ref[it : it + 1, :]
    rows_s[10:14, :] = bias_ref[it]
    columns = rows_s[...].T
    for d in range(9):
        coef_s[d] = jnp.broadcast_to(columns[:, d : d + 1], (LANES, LANES))
    for k in range(5):
        factor = 0.5 if k in (2, 3) else 1.0
        vec_s[k] = jnp.broadcast_to(columns[:, 9 + k : 10 + k] * factor, (LANES, LANES))


def load_weights(it, w_ref, m0_s, wg_s):
    def mat(k):
        return w_ref[it, k * LANES : (k + 1) * LANES, :].astype(F32).T

    m0_s[...] = mat(0).astype(BF16)
    h1, h2, h4, h5, h6 = (mat(k) * 0.5 for k in (1, 2, 4, 5, 6))
    parts = [
        jnp.concatenate([h1, h4], 1),
        jnp.concatenate([h2, h5], 1),
        jnp.concatenate([mat(3), h6], 1),
        jnp.concatenate([jnp.zeros_like(h6), h6], 1),
    ]
    for g in range(8):
        for n, part in enumerate(parts):
            wg_s[64 * g + 16 * n : 64 * g + 16 * n + 16, :] = part[16 * g : 16 * g + 16].astype(BF16)


def fill_row(ring, slot, row, west, east, lane):
    ring[slot, 1] = row
    ring[slot, 0] = jnp.where(lane == 0, west, pltpu.roll(row, 1, 1))
    ring[slot, 2] = jnp.where(lane == 127, east, pltpu.roll(row, 127, 1))


def fill_pole(ring, slot, line):
    wide = line.astype(F32)
    for b in range(3):
        ring[slot, b] = wide[1 + b : 129 + b].T


def fill_sides(side_s, west, east):
    side_s[0] = west.astype(F32).T
    side_s[1] = pltpu.roll(east.astype(F32).T, 127, 1)


def prep_block(g, read_row, ring, side_s, lane):
    for r in range(BLOCK):
        q = g * BLOCK + r
        turn = lax.rem(2 * LANES - q, LANES)
        row = read_row(q).astype(F32)
        fill_row(
            ring,
            lax.rem(q, DEPTH),
            row,
            pltpu.roll(side_s[0], turn, 1),
            pltpu.roll(side_s[1], turn, 1),
            lane,
        )


def stencil_block(g, ring, metric_ref, coef_s, vec_s, acc_s, write):
    for pair in range(BLOCK // 2):
        first = g * BLOCK + 2 * pair
        slots = [lax.rem(first + k - 1 + DEPTH, DEPTH) for k in range(4)]
        squares = [None, None]
        metric = [
            [jnp.broadcast_to(metric_ref[d, pl.ds(first + r, 1), :], (8, LANES)) for r in range(2)]
            for d in range(9)
        ]
        for group in range(LANES // 8):
            cs = slice(8 * group, 8 * group + 8)
            acc = [None, None]
            for k in range(4):
                for b in range(3):
                    cell = ring[slots[k], b, cs, :]
                    for a in range(3):
                        r = k - a
                        if 0 <= r < 2:
                            d = 3 * a + b
                            term = (cell * coef_s[d, cs, :]) * metric[d][r]
                            acc[r] = term if acc[r] is None else acc[r] + term
            for r in range(2):
                square = acc[r] * acc[r]
                squares[r] = square if squares[r] is None else squares[r] + square
                acc_s[cs, LANES * r : LANES * r + LANES] = acc[r]
        for r in range(2):
            mean = jnp.sum(squares[r], axis=0, keepdims=True) * (1.0 / LANES)
            scale = lax.rsqrt(mean + EPSILON)
            total = acc_s[:, LANES * r : LANES * r + LANES]
            write(2 * pair + r, (total * scale * vec_s[0]).astype(BF16))


def message_block(normed, m0_s, vec_s, write):
    product = jnp.dot(m0_s[...], normed, preferred_element_type=F32)
    for pair in range(BLOCK // 2):
        ls = slice(2 * LANES * pair, 2 * LANES * (pair + 1))
        write(ls, (product[:, ls] + twice(vec_s[1])).astype(BF16))


def gates_block(read_message, read_row, wg_s, vec_s, write):
    products = []
    for pair in range(BLOCK // 2):
        ls = slice(2 * LANES * pair, 2 * LANES * (pair + 1))
        current = jnp.concatenate([read_row(2 * pair), read_row(2 * pair + 1)], axis=1)
        both = jnp.concatenate([read_message(ls), current], axis=0)
        products.append((current, jnp.dot(wg_s[...], both, preferred_element_type=F32)))
    for pair in range(BLOCK // 2):
        current, w = products[pair]
        for g in range(8):
            o = 64 * g
            cs = slice(16 * g, 16 * g + 16)
            old = current[cs].astype(F32)
            update = jnp.tanh(w[o : o + 16] + twice(vec_s[2, cs, :]))
            reset = jnp.tanh(w[o + 16 : o + 32] + twice(vec_s[3, cs, :]))
            inner = (w[o + 32 : o + 48] + twice(vec_s[4, cs, :])) + reset * w[o + 48 : o + 64]
            new = jnp.tanh(inner)
            blend = ((old + new) + update * (old - new)) * 0.5
            blend = blend.astype(BF16)
            for r in range(2):
                write(2 * pair + r, cs, blend[:, LANES * r : LANES * r + LANES])


def run_stages(stages, order, first, last, count, guarded):
    def step(s, carry):
        for name in order:
            fn, lag = stages[name]
            if guarded:

                @pl.when((s >= lag) & (s - lag < count))
                def _():
                    fn(s - lag)

            else:
                fn(s - lag)
        return carry

    lax.fori_loop(first, last, step, 0)


def first_kernel(x_ref, metric_ref, north_ref, south_ref, west_ref, east_ref, coef_ref, gain_ref, bias_ref,
                 row_ref, normed_ref, ring, side_s, acc_s, rows_s, coef_s, vec_s):
    count = x_ref.shape[0] // BLOCK
    lane = lax.broadcasted_iota(jnp.int32, (LANES, LANES), 1)
    load_vectors(0, coef_ref, gain_ref, bias_ref, rows_s, coef_s, vec_s)
    fill_sides(side_s, west_ref[0], east_ref[0])
    fill_pole(ring, DEPTH - 1, north_ref[0])

    def read_row(q):
        row = x_ref[q].T
        row_ref[q] = row
        return row

    def prep(g):
        prep_block(g, read_row, ring, side_s, lane)

    def stencil(g):
        def write(r, normed):
            normed_ref[g * BLOCK + r] = normed

        stencil_block(g, ring, metric_ref, coef_s, vec_s, acc_s, write)

    prep(0)
    stages = {"P": (prep, 0), "S": (stencil, 1)}
    run_stages(stages, "PS", 1, count, count, False)
    fill_pole(ring, (count * BLOCK) % DEPTH, south_ref[0])
    stencil(count - 1)


def second_kernel(normed_ref, row_ref, metric_ref, lines_ref, sides_ref, coef_ref, gain_ref, bias_ref, w_ref,
                  out_ref, ring, state_s, side_s, acc_s, rows_s, coef_s, vec_s, old_vec_s, m0_s, wg_s,
                  msg1_s, msg2_s, normed_s, flip_s):
    count = out_ref.shape[0] // BLOCK
    lane = lax.broadcasted_iota(jnp.int32, (LANES, LANES), 1)
    load_vectors(0, coef_ref, gain_ref, bias_ref, rows_s, coef_s, old_vec_s)
    load_vectors(1, coef_ref, gain_ref, bias_ref, rows_s, coef_s, vec_s)
    for it in range(2):
        load_weights(it, w_ref, m0_s.at[it], wg_s.at[it])
    fill_sides(side_s, sides_ref[0], sides_ref[1])
    fill_pole(ring, DEPTH - 1, lines_ref[0])

    def message_one(g):
        buf = lax.rem(g, 2)
        normed = jnp.concatenate([normed_ref[g * BLOCK + r] for r in range(BLOCK)], axis=1)

        def write(ls, value):
            msg1_s[buf, :, ls] = value

        message_block(normed, m0_s.at[0], old_vec_s, write)

    def gates_one(g):
        buf = lax.rem(g, 2)

        def write(r, cs, value):
            state_s[lax.rem(g * BLOCK + r, 2 * DEPTH), cs, :] = value

        gates_block(lambda ls: msg1_s[buf, :, ls], lambda r: row_ref[g * BLOCK + r], wg_s.at[0], old_vec_s, write)

    def prep(g):
        prep_block(g, lambda q: state_s[lax.rem(q, 2 * DEPTH)], ring, side_s, lane)

    def stencil(g):
        buf = lax.rem(g, 2)

        def write(r, normed):
            normed_s[buf, :, LANES * r : LANES * r + LANES] = normed

        stencil_block(g, ring, metric_ref, coef_s, vec_s, acc_s, write)

    def message_two(g):
        buf = lax.rem(g, 2)

        def write(ls, value):
            msg2_s[buf, :, ls] = value

        message_block(normed_s[buf], m0_s.at[1], vec_s, write)

    def gates_two(g):
        buf = lax.rem(g, 2)

        def write(r, cs, value):
            flip_s[r, cs, :] = value

        gates_block(
            lambda ls: msg2_s[buf, :, ls],
            lambda r: state_s[lax.rem(g * BLOCK + r, 2 * DEPTH)],
            wg_s.at[1],
            vec_s,
            write,
        )
        for r in range(BLOCK):
            out_ref[g * BLOCK + r] = flip_s[r].T

    stages = {
        "m": (message_one, 0),
        "g": (gates_one, 1),
        "P": (prep, 2),
        "S": (stencil, 3),
        "M": (message_two, 4),
        "G": (gates_two, 5),
    }
    order = "PgGmMS"
    run_stages(stages, order, 0, 5, count, True)
    run_stages(stages, order, 5, count, count, False)
    fill_pole(ring, (count * BLOCK) % DEPTH, lines_ref[1])
    run_stages(stages, order, count, count + 5, count, True)


def ring_kernel(flags_ref, north_ref, south_ref, west_ref, east_ref, own_rows_ref, own_cols_ref,
                row_metric_ref, col_metric_ref, coef_ref, gain_ref, bias_ref, w_ref,
                lines_ref, sides_ref, line_s, new_s):
    polar = [flags_ref[0] == 1, flags_ref[1] == 1]
    ghost = [north_ref, south_ref]
    side = [west_ref, east_ref]

    def put(strip, n, value):
        line_s[strip, n, 8 : 8 + LINE, :] = value

    for e in range(2):
        outer = ghost[e][1].astype(F32)
        inner = own_rows_ref[e].astype(F32)
        before, after = (outer, inner) if e == 0 else (inner, outer)
        put(e, 0, jnp.where(polar[e], after, before))
        put(e, 1, ghost[e][0].astype(F32))
        put(e, 2, jnp.where(polar[e], before, after))
    for e in range(2):
        columns = [side[e][1], side[e][0], own_cols_ref[e]]
        if e == 1:
            columns = columns[::-1]
        for n in range(3):
            at = n if e == 0 else 129 + n
            line_s[2 + e, n, 0:8, :] = jnp.zeros((8, LANES), F32)
            line_s[2 + e, n, 136:152, :] = jnp.zeros((16, LANES), F32)
            line_s[2 + e, n, 10:138, :] = columns[n].astype(F32)
            line_s[2 + e, n, 9:10, :] = line_s[0, 1, 8 + at : 9 + at, :]
            line_s[2 + e, n, 138:139, :] = line_s[1, 1, 8 + at : 9 + at, :]
    normed = []
    old = []
    for strip in range(4):
        metric_ref = row_metric_ref if strip < 2 else col_metric_ref
        packed = metric_ref[strip % 2].astype(F32)
        metric = packed[:, 0:16] + packed[:, 16:32]
        total = None
        for n in range(3):
            for shift in range(3):
                d = 3 * n + shift if strip < 2 else 3 * shift + n
                cells = line_s[strip, n, 7 + shift : 7 + shift + LINE, :]
                term = metric[:, d : d + 1] * coef_ref[0, d : d + 1, :] * cells
                total = term if total is None else total + term
        scale = lax.rsqrt(jnp.mean(total * total, axis=1, keepdims=True) + EPSILON)
        normed.append(total * scale * gain_ref[0:1, :])
        old.append(line_s[strip, 1, 8 : 8 + LINE, :])
    normed = jnp.concatenate(normed, 0).astype(BF16)
    old = jnp.concatenate(old, 0)

    def mat(k):
        return w_ref[0, k * LANES : (k + 1) * LANES, :]

    def dot(a, k):
        return jnp.dot(a, mat(k), preferred_element_type=F32)

    message = (dot(normed, 0) + bias_ref[0, 0:1, :]).astype(BF16)
    hidden = old.astype(BF16)
    update = 0.5 * jnp.tanh(0.5 * (dot(message, 1) + dot(hidden, 4) + bias_ref[0, 1:2, :])) + 0.5
    reset = 0.5 * jnp.tanh(0.5 * (dot(message, 2) + dot(hidden, 5) + bias_ref[0, 2:3, :])) + 0.5
    new = jnp.tanh(dot(message, 3) + bias_ref[0, 3:4, :] + reset * dot(hidden, 6))
    new_s[...] = (1.0 - update) * new + update * old
    for e in range(2):
        lines_ref[e] = new_s[e * LINE : (e + 1) * LINE, :].astype(BF16)
        sides_ref[e] = new_s[(2 + e) * LINE + 2 : (2 + e) * LINE + 130, :].astype(BF16)


def call(kernel, name, outs, scratch, args, smem=0, flops=0, traffic=0):
    vmem = pl.BlockSpec(memory_space=pltpu.VMEM)
    scalar = pl.BlockSpec(memory_space=pltpu.SMEM)
    return pl.pallas_call(
        kernel,
        in_specs=[scalar] * smem + [vmem] * (len(args) - smem),
        out_specs=[vmem] * len(outs),
        out_shape=[jax.ShapeDtypeStruct(s, BF16) for s in outs],
        scratch_shapes=scratch,
        compiler_params=pltpu.CompilerParams(vmem_limit_bytes=40 * 1024 * 1024),
        cost_estimate=pl.CostEstimate(flops=flops, bytes_accessed=traffic, transcendentals=0),
        name=name,
    )(*args)


def split_metric(columns):
    high = lax.reduce_precision(columns, 8, 7)
    low = columns - high
    pad = ((0, 0), (0, 7))
    both = jnp.concatenate([jnp.pad(high, pad), jnp.pad(low, pad)], axis=1)
    return jnp.pad(both, ((0, 0), (0, LANES - 32))).astype(BF16)


def swap(mesh_shape, partner, value):
    lat, lon = mesh_shape
    pairs = [(i * lon + k, partner(i, k)[0] * lon + partner(i, k)[1]) for i in range(lat) for k in range(lon)]
    return lax.ppermute(value, ("lat", "lon"), pairs)


def on_device(state, edge_metric, stencil_coef, norm_gain, biases, weights):
    lat, lon = lax.axis_size("lat"), lax.axis_size("lon")
    shape = (lat, lon)
    half = lon // 2
    i, k = lax.axis_index("lat"), lax.axis_index("lon")
    rows, cols, channels = state.shape
    k_even = k % 2 == 0
    i_even = i % 2 == 0
    far = k >= half
    place = jnp.where(far, 2 * lat - 1 - i, i)

    def ordered(first, mine, theirs):
        return jnp.where(first, jnp.concatenate([mine, theirs]), jnp.concatenate([theirs, mine]))

    def halves(first, a, b):
        return jnp.where(first, a, b), jnp.where(first, b, a)

    shard = weights.transpose(1, 0, 2).reshape(-1, channels)

    col_w = jnp.stack([state[:, 0], state[:, 1]])
    col_e = jnp.stack([state[:, cols - 1], state[:, cols - 2]])
    met_w = split_metric(edge_metric[:, :, 0].T)
    met_e = split_metric(edge_metric[:, :, cols - 1].T)
    out_w = jnp.concatenate([col_w.reshape(-1, channels), met_w])
    out_e = jnp.concatenate([col_e.reshape(-1, channels), met_e])
    size = out_w.shape[0]
    send_near, send_far = halves(k_even, out_e, out_w)
    got_near = swap(shape, lambda i, k: (i, k ^ 1), jnp.concatenate([send_near, shard]))
    shard = ordered(k_even, shard, got_near[size:])
    got_far = swap(
        shape, lambda i, k: (i, (k + 1) % lon if k % 2 else (k - 1) % lon), jnp.concatenate([send_far, shard])
    )
    shard = ordered(jnp.logical_not(k_even), shard, got_far[size:])
    in_e, in_w = halves(k_even, got_near[:size], got_far[:size])
    ghost_w, ghost_e = (a[: 2 * rows].reshape(2, rows, channels) for a in (in_w, in_e))
    ghost_met_w, ghost_met_e = in_w[2 * rows :], in_e[2 * rows :]
    bit = 4
    while bit < half:
        got = swap(shape, lambda i, k, bit=bit: (i, k ^ bit), shard)
        shard = ordered((k & bit) == 0, shard, got)
        bit *= 2

    def extended(near, other):
        picked = jnp.stack([near, other])
        body = state[near : near + 1] if False else jnp.stack([state[near], state[other]])
        west = jnp.stack([ghost_w[1, near : near + 1], ghost_w[1, other : other + 1]])
        west1 = jnp.stack([ghost_w[0, near : near + 1], ghost_w[0, other : other + 1]])
        east1 = jnp.stack([ghost_e[0, near : near + 1], ghost_e[0, other : other + 1]])
        east = jnp.stack([ghost_e[1, near : near + 1], ghost_e[1, other : other + 1]])
        del picked
        fill = jnp.zeros((2, LINE - cols - 4, channels), BF16)
        return jnp.concatenate([west, west1, body, east1, east, fill], axis=1)

    def extended_metric(row):
        body = split_metric(edge_metric[:, row, :].T)
        zero = jnp.zeros((1, LANES), BF16)
        tail = jnp.zeros((LINE - cols - 3, LANES), BF16)
        return jnp.concatenate(
            [zero, ghost_met_w[row : row + 1], body, ghost_met_e[row : row + 1], tail]
        )

    row_n, row_s = extended(0, 1), extended(rows - 1, rows - 2)
    out_n = jnp.concatenate([row_n.reshape(-1, channels), extended_metric(0)])
    out_s = jnp.concatenate([row_s.reshape(-1, channels), extended_metric(rows - 1)])
    size = out_n.shape[0]
    send_a, send_b = halves(i_even, out_s, out_n)
    got_a = swap(shape, lambda i, k: (i ^ 1, k), jnp.concatenate([send_a, shard]))
    shard = ordered(place % 2 == 0, shard, got_a[size:])

    def across(i, k):
        if i == 0 or i == lat - 1:
            return i, (k + half) % lon
        return (i + 1, k) if i % 2 else (i - 1, k)

    got_b = swap(shape, across, jnp.concatenate([send_b, shard]))
    shard = ordered(place % 2 == 1, shard, got_b[size:])
    in_s, in_n = halves(i_even, got_a[:size], got_b[:size])
    ghost_n, ghost_s = (a[: 2 * LINE].reshape(2, LINE, channels) for a in (in_n, in_s))
    row_metric = jnp.stack([in_n[2 * LINE :], in_s[2 * LINE :]])

    def along(i, k, bit):
        m = (2 * lat - 1 - i if k >= half else i) ^ bit
        return (m, k % half) if m < lat else (2 * lat - 1 - m, k % half + half)

    bit = 4
    while bit < 2 * lat:
        got = swap(shape, lambda i, k, bit=bit: along(i, k, bit), shard)
        shard = ordered((place & bit) == 0, shard, got)
        bit *= 2

    def start(n):
        n = n % 4
        return jnp.where(n % 2 == 0, n - 2, n - 1)

    ring = jnp.roll(shard.reshape(2 * lat, -1), start(place), axis=0)
    ring = ring.reshape(2 * lat, half, -1)
    grid = jnp.concatenate([ring[:lat], ring[lat:][::-1]], axis=1)
    grid = jnp.roll(grid, start(k % half), axis=1)
    full = grid.reshape(-1, ITERS, channels).transpose(1, 0, 2)

    tile = state.shape
    square = (LANES, LANES)
    vmem = pltpu.VMEM
    row_t, normed = call(
        first_kernel,
        "aggregate",
        [tile, tile],
        [
            vmem((DEPTH, 3) + square, F32),
            vmem((2,) + square, F32),
            vmem((LANES, 2 * LANES), F32),
            vmem(square, F32),
            vmem((9,) + square, F32),
            vmem((5,) + square, F32),
        ],
        (state, edge_metric, ghost_n, ghost_s, ghost_w, ghost_e, stencil_coef, norm_gain, biases),
        flops=60 * state.size,
        traffic=8 * state.size,
    )
    pad = ((2, LINE - rows - 2), (0, 0))
    col_metric = jnp.stack([jnp.pad(ghost_met_w, pad), jnp.pad(ghost_met_e, pad)])
    flags = jnp.stack([i == 0, i == lat - 1]).astype(jnp.int32)
    lines, sides = call(
        ring_kernel,
        "border",
        [(2, LINE, channels), (2, rows, channels)],
        [vmem((4, 3, LINE + 16, LANES), F32), vmem((4 * LINE, LANES), F32)],
        (
            flags,
            ghost_n,
            ghost_s,
            ghost_w,
            ghost_e,
            jnp.stack([row_n[0], row_s[0]]),
            jnp.stack([col_w[0], col_e[0]]),
            row_metric,
            col_metric,
            stencil_coef,
            norm_gain,
            biases,
            full,
        ),
        smem=1,
    )
    (out,) = call(
        second_kernel,
        "refine",
        [tile],
        [
            vmem((DEPTH, 3) + square, F32),
            vmem((2 * DEPTH,) + square, BF16),
            vmem((2,) + square, F32),
            vmem((LANES, 2 * LANES), F32),
            vmem(square, F32),
            vmem((9,) + square, F32),
            vmem((5,) + square, F32),
            vmem((5,) + square, F32),
            vmem((2,) + square, BF16),
            vmem((2, 4 * LANES, 2 * LANES), BF16),
            vmem((2, LANES, BLOCK * LANES), BF16),
            vmem((2, LANES, BLOCK * LANES), BF16),
            vmem((2, LANES, BLOCK * LANES), BF16),
            vmem((BLOCK,) + square, BF16),
        ],
        (normed, row_t, edge_metric, lines, sides, stencil_coef, norm_gain, biases, full),
    )
    return out


def solution(mesh):
    in_specs = (
        P("lat", "lon", None),
        P(None, "lat", "lon"),
        P(),
        P(),
        P(),
        P(None, ("lat", "lon"), None),
    )
    out_specs = P("lat", "lon", None)
    return jax.shard_map(on_device, mesh=mesh, in_specs=in_specs, out_specs=out_specs, check_vma=False)
```

```python
import functools

import jax
import jax.numpy as jnp
from jax import lax
from jax.experimental import pallas as pl
from jax.experimental.pallas import tpu as pltpu
from jax.sharding import PartitionSpec as P

KMAT = 7
ITERS = 2
EPSILON = 1e-05
LANES = 128
BLOCK = 4
DEPTH = 4 * BLOCK
LINE = 136
ORDER_ONE = ("S", "PT")
ORDER_TWO = ("G", "M", "S", "P", "g", "m")
DELAY = 2
F32 = jnp.float32
BF16 = jnp.bfloat16


def twice(a):
    return jnp.concatenate([a, a], axis=1)


def load_vectors(it, coef_ref, gain_ref, bias_ref, rows_s, coef_s, vec_s):
    rows_s[...] = jnp.zeros_like(rows_s)
    rows_s[0:9, :] = coef_ref[it]
    rows_s[9:10, :] = gain_ref[it : it + 1, :]
    rows_s[10:14, :] = bias_ref[it]
    columns = rows_s[...].T
    for d in range(9):
        coef_s[d] = jnp.broadcast_to(columns[:, d : d + 1], (LANES, LANES))
    for k in range(5):
        factor = 0.5 if k in (2, 3) else 1.0
        vec_s[k] = jnp.broadcast_to(columns[:, 9 + k : 10 + k] * factor, (LANES, LANES))


def load_weights(it, w_ref, m0_s, wg_s):
    def mat(k):
        return w_ref[it, k * LANES : (k + 1) * LANES, :].astype(F32).T

    m0_s[...] = mat(0).astype(BF16)
    h1, h2, h4, h5, h6 = (mat(k) * 0.5 for k in (1, 2, 4, 5, 6))
    parts = [
        jnp.concatenate([h1, h4], 1),
        jnp.concatenate([h2, h5], 1),
        jnp.concatenate([mat(3), h6], 1),
        jnp.concatenate([jnp.zeros_like(h6), h6], 1),
    ]
    for g in range(8):
        for n, part in enumerate(parts):
            wg_s[64 * g + 16 * n : 64 * g + 16 * n + 16, :] = part[16 * g : 16 * g + 16].astype(BF16)


def fill_pole(ring, slot, line):
    wide = line.astype(F32)
    for b in range(3):
        ring[slot, b] = wide[1 + b : 129 + b].T


def fill_sides(side_s, west, east):
    odd = lax.broadcasted_iota(jnp.int32, (LANES, LANES), 1) % 2 == 1
    west = west.astype(F32).T
    east = pltpu.roll(east.astype(F32).T, 127, 1)
    side_s[0] = jnp.where(odd, east, west).astype(BF16)
    side_s[1] = jnp.where(odd, west, east).astype(BF16)


def prep_block(g, read_part, ring, side_s, lane):
    pending = []

    def put():
        slot, cs, planes = pending.pop(0)
        for b, plane in enumerate(planes):
            ring[slot, b, cs, :] = plane.astype(F32)

    for r in range(BLOCK):
        q = g * BLOCK + r
        slot = lax.rem(q, ring.shape[0])
        turn = lax.rem(2 * LANES - q, LANES)
        for n in range(LANES // 16):
            cs = slice(16 * n, 16 * n + 16)
            part = read_part(q, cs)
            side = pltpu.roll(side_s[r % 2, cs, :], turn, 1)
            west = jnp.where(lane == 0, side, pltpu.roll(part, 1, 1))
            east = jnp.where(lane == 127, side, pltpu.roll(part, 127, 1))
            pending.append((slot, cs, (west, part, east)))
            if len(pending) > DELAY:
                put()
            yield
    while pending:
        put()


def stencil_block(g, ring, metric_ref, coef_s, vec_s, acc_s, write):
    for pair in range(BLOCK // 2):
        first = g * BLOCK + 2 * pair
        depth = ring.shape[0]
        slots = [lax.rem(first + k - 1 + depth, depth) for k in range(4)]
        squares = [None, None]
        metric = [
            [jnp.broadcast_to(metric_ref[d, pl.ds(first + r, 1), :], (8, LANES)) for r in range(2)]
            for d in range(9)
        ]
        for group in range(LANES // 8):
            cs = slice(8 * group, 8 * group + 8)
            acc = [None, None]
            for k in range(4):
                for b in range(3):
                    cell = ring[slots[k], b, cs, :]
                    for a in range(3):
                        r = k - a
                        if 0 <= r < 2:
                            d = 3 * a + b
                            term = (cell * coef_s[d, cs, :]) * metric[d][r]
                            acc[r] = term if acc[r] is None else acc[r] + term
            for r in range(2):
                square = acc[r] * acc[r]
                squares[r] = square if squares[r] is None else squares[r] + square
                acc_s[cs, LANES * r : LANES * r + LANES] = acc[r]
            yield
        for r in range(2):
            mean = jnp.sum(squares[r], axis=0, keepdims=True) * (1.0 / LANES)
            scale = lax.rsqrt(mean + EPSILON)
            total = acc_s[:, LANES * r : LANES * r + LANES]
            write(2 * pair + r, (total * scale * vec_s[0]).astype(BF16))


def message_block(normed, m0_s, vec_s, write):
    product = jnp.dot(m0_s[...], normed, preferred_element_type=F32)
    for pair in range(BLOCK // 2):
        ls = slice(2 * LANES * pair, 2 * LANES * (pair + 1))
        write(ls, (product[:, ls] + twice(vec_s[1])).astype(BF16))
        yield


def gates_block(read_message, read_row, wg_s, vec_s, write):
    products = []
    for pair in range(BLOCK // 2):
        ls = slice(2 * LANES * pair, 2 * LANES * (pair + 1))
        current = jnp.concatenate([read_row(2 * pair), read_row(2 * pair + 1)], axis=1)
        both = jnp.concatenate([read_message(ls), current], axis=0)
        products.append((current, jnp.dot(wg_s[...], both, preferred_element_type=F32)))
    for pair in range(BLOCK // 2):
        current, w = products[pair]
        for g in range(8):
            o = 64 * g
            cs = slice(16 * g, 16 * g + 16)
            old = current[cs].astype(F32)
            update = jnp.tanh(w[o : o + 16] + twice(vec_s[2, cs, :]))
            reset = jnp.tanh(w[o + 16 : o + 32] + twice(vec_s[3, cs, :]))
            inner = (w[o + 32 : o + 48] + twice(vec_s[4, cs, :])) + reset * w[o + 48 : o + 64]
            new = jnp.tanh(inner)
            blend = ((old + new) + update * (old - new)) * 0.5
            blend = blend.astype(BF16)
            for r in range(2):
                write(2 * pair + r, cs, blend[:, LANES * r : LANES * r + LANES])
            yield


def weave(parts):
    live = [[part, size, 0] for part, size in parts]
    while live:
        live.sort(key=lambda t: (t[2] + 0.5) / t[1])
        turn = live[0]
        turn[2] += 1
        if next(turn[0], True):
            live.remove(turn)


def run_stages(stages, order, first, last, guarded):
    def step(s, carry):
        for word in order:
            if guarded:
                for name in word:
                    fn, lag, size, low, high = stages[name]

                    @pl.when((s >= lag + low) & (s < lag + high))
                    def _():
                        weave([(fn(s - lag), size)])

            else:
                weave([(stages[name][0](s - stages[name][1]), stages[name][2]) for name in word])
        return carry

    lax.fori_loop(first, last, step, 0)


def first_kernel(begin, end, before, wrap, *refs):
    x_ref, metric_ref, west_ref, east_ref, coef_ref, gain_ref, bias_ref = refs[:7]
    rest = refs[7:]
    if wrap:
        north_ref, south_ref = rest[:2]
        rest = rest[2:]
    if before:
        old_row_ref, old_normed_ref = rest[:2]
        rest = rest[2:]
    row_ref, normed_ref, ring, side_s, acc_s, rows_s, coef_s, vec_s = rest
    lane = lax.broadcasted_iota(jnp.int32, (16, LANES), 1)
    load_vectors(0, coef_ref, gain_ref, bias_ref, rows_s, coef_s, vec_s)
    fill_sides(side_s, west_ref[...], east_ref[...])

    def turn(g):
        for r in range(BLOCK):
            row = x_ref[g * BLOCK + r].T
            yield
            row_ref[g * BLOCK + r] = row
            yield

    def prep(g):
        yield from prep_block(g, lambda q, cs: row_ref[q, cs, :], ring, side_s, lane)

    def stencil(g):
        def write(r, normed):
            normed_ref[g * BLOCK + r] = normed

        yield from stencil_block(g, ring, metric_ref, coef_s, vec_s, acc_s, write)

    def copy(g, carry):
        for r in range(BLOCK):
            row_ref[g * BLOCK + r] = old_row_ref[g * BLOCK + r]
            normed_ref[g * BLOCK + r] = old_normed_ref[g * BLOCK + r]
        return carry

    count = x_ref.shape[0] // BLOCK

    def span(lo, hi):
        low, high = max(lo - 1, 0), min(hi + 1, count)
        stages = {
            "T": (turn, 0, 8, low, high),
            "P": (prep, 1, 32, low, high),
            "S": (stencil, 3, 32, lo, hi),
        }
        if lo == 0:
            fill_pole(ring, DEPTH - 1, north_ref[...])
        run_stages(stages, ("P", "T"), low, lo + 3, True)
        full = min(high, hi + 3)
        run_stages(stages, ORDER_ONE, lo + 3, full, False)
        if hi == count:
            fill_pole(ring, (count * BLOCK) % DEPTH, south_ref[...])
        run_stages(stages, ("S", "P"), full, hi + 3, True)

    if before:
        lax.fori_loop(1, 1 + before, copy, 0)
    if wrap:
        span(0, 1)
    span(begin, end)


def second_kernel(normed_ref, row_ref, metric_ref, lines_ref, sides_ref, coef_ref, gain_ref, bias_ref, w_ref,
                  out_ref, ring, state_s, side_s, acc_s, rows_s, coef_s, vec_s, old_vec_s, m0_s, wg_s,
                  msg1_s, msg2_s, normed_s, flip_s):
    count = out_ref.shape[0] // BLOCK
    lane = lax.broadcasted_iota(jnp.int32, (16, LANES), 1)
    load_vectors(0, coef_ref, gain_ref, bias_ref, rows_s, coef_s, old_vec_s)
    load_vectors(1, coef_ref, gain_ref, bias_ref, rows_s, coef_s, vec_s)
    for it in range(2):
        load_weights(it, w_ref, m0_s.at[it], wg_s.at[it])
    fill_sides(side_s, sides_ref[0], sides_ref[1])
    fill_pole(ring, 2 * DEPTH - 1, lines_ref[0])

    def message_one(g):
        buf = lax.rem(g, 2)
        normed = jnp.concatenate([normed_ref[g * BLOCK + r] for r in range(BLOCK)], axis=1)

        def write(ls, value):
            msg1_s[buf, :, ls] = value

        yield from message_block(normed, m0_s.at[0], old_vec_s, write)

    def gates_one(g):
        buf = lax.rem(g, 2)

        def write(r, cs, value):
            state_s[lax.rem(g * BLOCK + r, 2 * DEPTH), cs, :] = value

        yield from gates_block(lambda ls: msg1_s[buf, :, ls], lambda r: row_ref[g * BLOCK + r], wg_s.at[0], old_vec_s, write)

    def prep(g):
        yield from prep_block(g, lambda q, cs: state_s[lax.rem(q, 2 * DEPTH), cs, :], ring, side_s, lane)

    def stencil(g):
        buf = lax.rem(g, 2)

        def write(r, normed):
            normed_s[buf, :, LANES * r : LANES * r + LANES] = normed

        yield from stencil_block(g, ring, metric_ref, coef_s, vec_s, acc_s, write)

    def message_two(g):
        buf = lax.rem(g, 2)

        def write(ls, value):
            msg2_s[buf, :, ls] = value

        yield from message_block(normed_s[buf], m0_s.at[1], vec_s, write)

    def gates_two(g):
        buf = lax.rem(g, 2)

        def write(r, cs, value):
            flip_s[r, cs, :] = value

        yield from gates_block(
            lambda ls: msg2_s[buf, :, ls],
            lambda r: state_s[lax.rem(g * BLOCK + r, 2 * DEPTH)],
            wg_s.at[1],
            vec_s,
            write,
        )
        for r in range(BLOCK):
            out_ref[g * BLOCK + r] = flip_s[r].T

    stages = {
        "m": (message_one, 0, 2, 0, count),
        "g": (gates_one, 1, 16, 0, count),
        "P": (prep, 2, 32, 0, count),
        "S": (stencil, 4, 32, 0, count),
        "M": (message_two, 5, 2, 0, count),
        "G": (gates_two, 6, 16, 0, count),
    }
    run_stages(stages, ORDER_TWO, 0, 6, True)
    run_stages(stages, ORDER_TWO, 6, count, False)
    fill_pole(ring, (count * BLOCK) % (2 * DEPTH), lines_ref[1])
    run_stages(stages, ORDER_TWO, count, count + 6, True)


def ring_kernel(flags_ref, north_ref, south_ref, west_ref, east_ref, own_rows_ref, own_cols_ref,
                row_metric_ref, col_metric_ref, coef_ref, gain_ref, bias_ref, w_ref,
                lines_ref, sides_ref, line_s, metric_s, new_s):
    polar = [flags_ref[0] == 1, flags_ref[1] == 1]
    ghost = [north_ref, south_ref]
    side = [west_ref, east_ref]

    def put(strip, n, value):
        line_s[strip, n, 8 : 8 + LINE, :] = value

    for e in range(2):
        outer = ghost[e][1].astype(F32)
        inner = own_rows_ref[e].astype(F32)
        before, after = (outer, inner) if e == 0 else (inner, outer)
        put(e, 0, jnp.where(polar[e], after, before))
        put(e, 1, ghost[e][0].astype(F32))
        put(e, 2, jnp.where(polar[e], before, after))
    for e in range(2):
        columns = [side[e][0], side[e][1], own_cols_ref[e]] if e == 0 else [side[e][1], side[e][0], own_cols_ref[e]]
        if e == 1:
            columns = columns[::-1]
        for n in range(3):
            at = n if e == 0 else 129 + n
            line_s[2 + e, n, 0:8, :] = jnp.zeros((8, LANES), F32)
            line_s[2 + e, n, 136:152, :] = jnp.zeros((16, LANES), F32)
            line_s[2 + e, n, 10:138, :] = columns[n].astype(F32)
            line_s[2 + e, n, 9:10, :] = line_s[0, 1, 8 + at : 9 + at, :]
            line_s[2 + e, n, 138:139, :] = line_s[1, 1, 8 + at : 9 + at, :]

    def upright(packed):
        both = packed.astype(F32)
        tall = jnp.concatenate([both[0:16] + both[16:32], jnp.zeros((LANES - 16, LANES), F32)], axis=0)
        return tall.T

    metric_s[...] = jnp.zeros_like(metric_s)
    for e in range(2):
        metric_s[e, 2:130, :] = upright(row_metric_ref[e, 0:32])
        ends = upright(row_metric_ref[e, 32:64])
        metric_s[e, 1:2, :] = ends[0:1]
        metric_s[e, 130:131, :] = ends[1:2]
        metric_s[2 + e, 2:130, :] = upright(col_metric_ref[e])
    normed = []
    old = []
    for strip in range(4):
        metric = metric_s[strip]
        total = None
        for n in range(3):
            for shift in range(3):
                d = 3 * n + shift if strip < 2 else 3 * shift + n
                cells = line_s[strip, n, 7 + shift : 7 + shift + LINE, :]
                term = metric[:, d : d + 1] * coef_ref[0, d : d + 1, :] * cells
                total = term if total is None else total + term
        scale = lax.rsqrt(jnp.mean(total * total, axis=1, keepdims=True) + EPSILON)
        normed.append(total * scale * gain_ref[0:1, :])
        old.append(line_s[strip, 1, 8 : 8 + LINE, :])
    normed = jnp.concatenate(normed, 0).astype(BF16)
    old = jnp.concatenate(old, 0)

    def mat(k):
        return w_ref[0, k * LANES : (k + 1) * LANES, :]

    def dot(a, k):
        return jnp.dot(a, mat(k), preferred_element_type=F32)

    message = (dot(normed, 0) + bias_ref[0, 0:1, :]).astype(BF16)
    hidden = old.astype(BF16)
    update = 0.5 * jnp.tanh(0.5 * (dot(message, 1) + dot(hidden, 4) + bias_ref[0, 1:2, :])) + 0.5
    reset = 0.5 * jnp.tanh(0.5 * (dot(message, 2) + dot(hidden, 5) + bias_ref[0, 2:3, :])) + 0.5
    new = jnp.tanh(dot(message, 3) + bias_ref[0, 3:4, :] + reset * dot(hidden, 6))
    new_s[...] = (1.0 - update) * new + update * old
    for e in range(2):
        lines_ref[e] = new_s[e * LINE : (e + 1) * LINE, :].astype(BF16)
        sides_ref[e] = new_s[(2 + e) * LINE + 2 : (2 + e) * LINE + 130, :].astype(BF16)


def call(kernel, name, outs, scratch, args, smem=0, flops=0, traffic=0, limit=24):
    vmem = pl.BlockSpec(memory_space=pltpu.VMEM)
    scalar = pl.BlockSpec(memory_space=pltpu.SMEM)
    return pl.pallas_call(
        kernel,
        in_specs=[scalar] * smem + [vmem] * (len(args) - smem),
        out_specs=[vmem] * len(outs),
        out_shape=[jax.ShapeDtypeStruct(s, BF16) for s in outs],
        scratch_shapes=scratch,
        compiler_params=pltpu.CompilerParams(vmem_limit_bytes=limit * 1024 * 1024),
        cost_estimate=pl.CostEstimate(flops=flops, bytes_accessed=traffic, transcendentals=0),
        name=name,
    )(*args)


def split_metric(values):
    high = lax.reduce_precision(values, 8, 7)
    pad = ((0, 7), (0, 0))
    return jnp.concatenate([jnp.pad(high, pad), jnp.pad(values - high, pad)]).astype(BF16)


def swap(mesh_shape, partner, value):
    lat, lon = mesh_shape
    pairs = [(i * lon + k, partner(i, k)[0] * lon + partner(i, k)[1]) for i in range(lat) for k in range(lon)]
    return lax.ppermute(value, ("lat", "lon"), pairs)


def on_device(state, edge_metric, stencil_coef, norm_gain, biases, weights):
    lat, lon = lax.axis_size("lat"), lax.axis_size("lon")
    shape = (lat, lon)
    half = lon // 2
    i, k = lax.axis_index("lat"), lax.axis_index("lon")
    rows, cols, channels = state.shape
    k_even = k % 2 == 0
    i_even = i % 2 == 0

    def ordered(first, mine, theirs):
        return jnp.where(first, jnp.concatenate([mine, theirs]), jnp.concatenate([theirs, mine]))

    def halves(first, a, b):
        return jnp.where(first, a, b), jnp.where(first, b, a)

    def after(value, *others):
        return lax.optimization_barrier((value,) + others)[0]

    shard = weights.transpose(1, 0, 2).reshape(-1, channels)

    def edge(east):
        first = jnp.where(east, cols - 2, 0)
        last = jnp.where(east, cols - 1, 0)
        columns = lax.dynamic_slice(state, (0, first, 0), (rows, 2, channels)).transpose(1, 0, 2)
        metric = lax.dynamic_slice(edge_metric, (0, 0, last), (9, rows, 1)).reshape(9, rows)
        return columns.reshape(-1, channels), split_metric(metric)

    near, near_metric = edge(k_even)
    got_near = swap(shape, lambda i, k: (i, k ^ 1), jnp.concatenate([near, near_metric, shard]))
    far, far_metric = edge(jnp.logical_not(k_even))
    size = 2 * rows + 32
    shard = ordered(k_even, shard, got_near[size:])
    got_far = swap(
        shape,
        lambda i, k: (i, (k + 1) % lon if k % 2 else (k - 1) % lon),
        jnp.concatenate([far, far_metric, shard]),
    )
    shard = ordered(jnp.logical_not(k_even), shard, got_far[size:])
    in_e, in_w = halves(k_even, got_near[:size], got_far[:size])
    ghost_w, ghost_e = (a[: 2 * rows].reshape(2, rows, channels) for a in (in_w, in_e))
    metric_w, metric_e = in_w[2 * rows :], in_e[2 * rows :]
    own_e, own_w = halves(k_even, near, far)

    def extended(row, inner):
        lines = []
        for q in (row, inner):
            fill = jnp.zeros((LINE - cols - 4, channels), BF16)
            lines.append(jnp.concatenate([ghost_w[:, q], state[q], ghost_e[:, q], fill]))
        return jnp.stack(lines)

    def extended_metric(row):
        ends = jnp.concatenate([metric_w[:, row : row + 1], metric_e[:, row : row + 1]], axis=1)
        ends = jnp.pad(ends, ((0, 0), (0, LANES - 2)))
        return jnp.concatenate([split_metric(edge_metric[:, row]), ends])

    row_n, row_s = extended(0, 1), extended(rows - 1, rows - 2)
    out_n = jnp.concatenate([row_n.reshape(-1, channels), extended_metric(0)])
    out_s = jnp.concatenate([row_s.reshape(-1, channels), extended_metric(rows - 1)])
    size = out_n.shape[0]
    send_a, send_b = halves(i_even, out_s, out_n)
    send_a = jnp.concatenate([send_a, shard])

    def across(i, k):
        if i == 0 or i == lat - 1:
            return i, (k + half) % lon
        return (i + 1, k) if i % 2 else (i - 1, k)

    got_a = swap(shape, lambda i, k: (i ^ 1, k), send_a)
    got_b = swap(shape, across, send_b)

    tile = state.shape
    square = (LANES, LANES)
    vmem = pltpu.VMEM
    count = rows // BLOCK
    cuts = [1, 1 + (count - 1) // 3, 1 + 2 * (count - 1) // 3, count]

    def aggregate(part, side_w, more):
        begin, end = cuts[part], cuts[part + 1]
        return call(
            functools.partial(first_kernel, begin, end, begin - 1, part == 2),
            "aggregate%d" % part,
            [tile, tile],
            [
                vmem((DEPTH, 3) + square, F32),
                vmem((2,) + square, BF16),
                vmem((LANES, 2 * LANES), F32),
                vmem(square, F32),
                vmem((9,) + square, F32),
                vmem((5,) + square, F32),
            ],
            (state, edge_metric, side_w, ghost_e[0], stencil_coef, norm_gain, biases) + more,
            flops=20 * state.size,
            traffic=8 * state.size,
        )

    held = aggregate(0, after(ghost_w[1], send_a, send_b), ())

    shard = ordered((i & 1) == 0, shard, got_a[size:])
    in_s, in_n = halves(i_even, got_a[:size], got_b)
    ghost_n, ghost_s = (a[: 2 * LINE].reshape(2, LINE, channels) for a in (in_n, in_s))
    row_metric = jnp.stack([in_n[2 * LINE :], in_s[2 * LINE :]])

    shard = shard.reshape(2, 4, -1, channels)
    bit = 4
    while bit < lon:
        mine = after(shard, *held) if bit == 4 else shard
        got = swap(shape, lambda i, k, bit=bit: (i, k ^ bit), mine)
        low = (k & bit) == 0
        shard = jnp.where(
            low, jnp.concatenate([shard, got], axis=1), jnp.concatenate([got, shard], axis=1)
        )
        if bit == 4:
            held = aggregate(1, after(ghost_w[1], mine), tuple(held))
        bit *= 2
    place = k % 4
    shard = jnp.where(
        place == 0,
        jnp.roll(shard, -2, axis=1),
        jnp.where(place == 3, jnp.roll(shard, 2, axis=1), shard),
    )
    shard = shard.reshape(-1, channels)
    bit = 2
    while bit < lat:
        mine = after(shard, *held) if bit == 2 else shard
        got = swap(shape, lambda i, k, bit=bit: (i ^ bit, k), mine)
        shard = ordered((i & bit) == 0, shard, got)
        if bit == 2:
            held = aggregate(2, after(ghost_w[1], mine), (ghost_n[0], ghost_s[0]) + tuple(held))
        bit *= 2
    row_t, normed = held
    full = shard.reshape(-1, ITERS, channels).transpose(1, 0, 2)

    flags = jnp.stack([i == 0, i == lat - 1]).astype(jnp.int32)
    lines, sides = call(
        ring_kernel,
        "border",
        [(2, LINE, channels), (2, rows, channels)],
        [vmem((4, 3, LINE + 16, LANES), F32), vmem((4, LINE, LANES), F32), vmem((4 * LINE, LANES), F32)],
        (
            flags,
            ghost_n,
            ghost_s,
            ghost_w,
            ghost_e,
            jnp.stack([row_n[0], row_s[0]]),
            jnp.stack([own_w[:rows], own_e[rows:]]),
            row_metric,
            jnp.stack([metric_w, metric_e]),
            stencil_coef,
            norm_gain,
            biases,
            full,
        ),
        smem=1,
        limit=12,
    )
    (out,) = call(
        second_kernel,
        "refine",
        [tile],
        [
            vmem((2 * DEPTH, 3) + square, F32),
            vmem((2 * DEPTH,) + square, BF16),
            vmem((2,) + square, BF16),
            vmem((LANES, 2 * LANES), F32),
            vmem(square, F32),
            vmem((9,) + square, F32),
            vmem((5,) + square, F32),
            vmem((5,) + square, F32),
            vmem((2,) + square, BF16),
            vmem((2, 4 * LANES, 2 * LANES), BF16),
            vmem((2, LANES, BLOCK * LANES), BF16),
            vmem((2, LANES, BLOCK * LANES), BF16),
            vmem((2, LANES, BLOCK * LANES), BF16),
            vmem((BLOCK,) + square, BF16),
        ],
        (normed, row_t, edge_metric, lines, sides, stencil_coef, norm_gain, biases, full),
    )
    return out


def solution(mesh):
    in_specs = (
        P("lat", "lon", None),
        P(None, "lat", "lon"),
        P(),
        P(),
        P(),
        P(None, ("lat", "lon"), None),
    )
    out_specs = P("lat", "lon", None)
    return jax.shard_map(on_device, mesh=mesh, in_specs=in_specs, out_specs=out_specs, check_vma=False)
```

```python
import functools

import jax
import jax.numpy as jnp
from jax import lax
from jax.experimental import pallas as pl
from jax.experimental.pallas import tpu as pltpu
from jax.sharding import PartitionSpec as P

KMAT = 7
ITERS = 2
EPSILON = 1e-05
LANES = 128
BLOCK = 4
DEPTH = 4 * BLOCK
LINE = 136
ORDER_ONE = (("S", 0), ("T", 0))
ORDER_TWO = (("G", 99), ("M", 99), ("S", 99), ("g", 99), ("m", 99), ("O", 99))
F32 = jnp.float32
BF16 = jnp.bfloat16


def twice(a):
    return jnp.concatenate([a, a], axis=1)


def load_vectors(it, coef_ref, gain_ref, bias_ref, rows_s, coef_s, vec_s):
    rows_s[...] = jnp.zeros_like(rows_s)
    rows_s[0:9, :] = coef_ref[:, it, :]
    rows_s[9:10, :] = gain_ref[it : it + 1, :]
    rows_s[10:14, :] = bias_ref[it]
    columns = rows_s[...].T
    for d in range(9):
        coef_s[d] = jnp.broadcast_to(columns[:, d : d + 1], (LANES, LANES))
    for k in range(5):
        factor = 0.5 if k in (2, 3) else 1.0
        vec_s[k] = jnp.broadcast_to(columns[:, 9 + k : 10 + k] * factor, (LANES, LANES))


def load_weights(it, w_ref, m0_s, wg_s):
    def mat(k):
        return w_ref[it, k * LANES : (k + 1) * LANES, :].astype(F32).T

    m0_s[...] = mat(0).astype(BF16)
    h1, h2, h4, h5, h6 = (mat(k) * 0.5 for k in (1, 2, 4, 5, 6))
    parts = [
        jnp.concatenate([h1, h4], 1),
        jnp.concatenate([h2, h5], 1),
        jnp.concatenate([mat(3), h6], 1),
        jnp.concatenate([jnp.zeros_like(h6), h6], 1),
    ]
    for g in range(8):
        for n, part in enumerate(parts):
            wg_s[64 * g + 16 * n : 64 * g + 16 * n + 16, :] = part[16 * g : 16 * g + 16].astype(BF16)


def turned_lines(line):
    wide = line.astype(F32)
    return [wide[1 + b : 129 + b].T for b in range(3)]


def fill_sides(side_s, west, east, side_metric_ref, coef_s, north, south):
    lane = lax.broadcasted_iota(jnp.int32, (LANES, LANES), 1)

    def part(side, column, above, below):
        middle = side.astype(F32).T
        upper, lower = pltpu.roll(middle, 1, 1), pltpu.roll(middle, LANES - 1, 1)
        if above is not None:
            upper = jnp.where(lane == 0, above, upper)
            lower = jnp.where(lane == LANES - 1, below, lower)
        total = None
        for a, cells in enumerate((upper, middle, lower)):
            d = 3 * a + 2 * column
            term = (cells * coef_s[d]) * side_metric_ref[column, d : d + 1, :]
            total = term if total is None else total + term
        return total

    ends = [None] * 4
    if north is not None:
        ends = [north[0][:, 0:1], south[0][:, 0:1], north[2][:, LANES - 1 :], south[2][:, LANES - 1 :]]
    first = part(west, 0, ends[0], ends[1])
    last = pltpu.roll(part(east, 1, ends[2], ends[3]), LANES - 1, 1)
    odd = lane % 2 == 1
    side_s[0] = jnp.where(odd, last, first)
    side_s[1] = jnp.where(odd, first, last)


def stencil_block(g, read_part, metric_ref, side_s, coef_s, vec_s, acc_s, lane, write):
    for pair in range(BLOCK // 2):
        first = g * BLOCK + 2 * pair
        squares = [None, None]
        turns = [lax.rem(2 * LANES - first - r, LANES) for r in range(2)]
        metric = [
            [jnp.broadcast_to(metric_ref[d, pl.ds(first + r, 1), :], (8, LANES)) for r in range(2)]
            for d in range(9)
        ]
        for group in range(LANES // 16):
            rows = [read_part(first - 1 + k, slice(16 * group, 16 * group + 16)).astype(F32) for k in range(4)]
            for half in range(2):
                cs = slice(16 * group + 8 * half, 16 * group + 8 * half + 8)
                cells = [row[8 * half : 8 * half + 8] for row in rows]
                for r in range(2):
                    sums = []
                    for b in range(3):
                        total = None
                        for a in range(3):
                            d = 3 * a + b
                            term = (cells[r + a] * coef_s[d, cs, :]) * metric[d][r]
                            total = term if total is None else total + term
                        sums.append(total)
                    side = pltpu.roll(side_s[r, cs, :], turns[r], 1)
                    west = jnp.where(lane == 0, side, pltpu.roll(sums[0], 1, 1))
                    east = jnp.where(lane == LANES - 1, side, pltpu.roll(sums[2], LANES - 1, 1))
                    total = (sums[1] + west) + east
                    square = total * total
                    squares[r] = square if squares[r] is None else squares[r] + square
                    acc_s[cs, LANES * r : LANES * r + LANES] = total
                yield
        for r in range(2):
            mean = jnp.sum(squares[r], axis=0, keepdims=True) * (1.0 / LANES)
            scale = lax.rsqrt(mean + EPSILON)
            total = acc_s[:, LANES * r : LANES * r + LANES]
            write(2 * pair + r, (total * scale * vec_s[0]).astype(BF16))


def message_block(normed, m0_s, vec_s, write):
    product = jnp.dot(m0_s[...], normed, preferred_element_type=F32)
    yield
    for pair in range(BLOCK // 2):
        ls = slice(2 * LANES * pair, 2 * LANES * (pair + 1))
        write(ls, (product[:, ls] + twice(vec_s[1])).astype(BF16))
        yield


def gates_block(read_message, read_part, wg_s, vec_s, write):
    products = []
    for pair in range(BLOCK // 2):
        ls = slice(2 * LANES * pair, 2 * LANES * (pair + 1))
        whole = slice(0, LANES)
        current = jnp.concatenate([read_part(2 * pair, whole), read_part(2 * pair + 1, whole)], axis=1)
        both = jnp.concatenate([read_message(ls), current], axis=0)
        products.append(jnp.dot(wg_s[...], both, preferred_element_type=F32))
    yield
    for pair in range(BLOCK // 2):
        w = products[pair]
        for g in range(8):
            o = 64 * g
            cs = slice(16 * g, 16 * g + 16)
            old = jnp.concatenate([read_part(2 * pair, cs), read_part(2 * pair + 1, cs)], axis=1).astype(F32)
            update = jnp.tanh(w[o : o + 16] + twice(vec_s[2, cs, :]))
            reset = jnp.tanh(w[o + 16 : o + 32] + twice(vec_s[3, cs, :]))
            inner = (w[o + 32 : o + 48] + twice(vec_s[4, cs, :])) + reset * w[o + 48 : o + 64]
            new = jnp.tanh(inner)
            blend = ((old + new) + update * (old - new)) * 0.5
            blend = blend.astype(BF16)
            for r in range(2):
                write(2 * pair + r, cs, blend[:, LANES * r : LANES * r + LANES])
            yield


def run_stages(stages, order, first, last, guarded):
    names = list(dict.fromkeys(name for name, _ in order))

    def step(s, carry):
        if guarded:
            for name in names:
                fn, lag, low, high = stages[name]

                @pl.when((s >= lag + low) & (s < lag + high))
                def _():
                    for _ in fn(s - lag):
                        pass

            return carry
        parts = {name: stages[name][0](s - stages[name][1]) for name in names}
        for name, pieces in order:
            for _ in range(pieces):
                next(parts[name], None)
        for name in names:
            for _ in parts[name]:
                pass
        return carry

    lax.fori_loop(first, last, step, 0)


def first_kernel(begin, end, before, wrap, *refs):
    x_ref, metric_ref, side_metric_ref, west_ref, east_ref, coef_ref, gain_ref, bias_ref = refs[:8]
    rest = refs[8:]
    if wrap:
        north_ref, south_ref = rest[:2]
        rest = rest[2:]
    if before:
        old_row_ref, old_normed_ref = rest[:2]
        rest = rest[2:]
    row_ref, normed_ref, side_s, acc_s, rows_s, coef_s, vec_s = rest
    lane = lax.broadcasted_iota(jnp.int32, (8, LANES), 1)
    count = x_ref.shape[0] // BLOCK
    load_vectors(0, coef_ref, gain_ref, bias_ref, rows_s, coef_s, vec_s)
    north = south = None
    if wrap:
        north, south = turned_lines(north_ref[...]), turned_lines(south_ref[...])
        row_ref[BLOCK - 1] = north[1].astype(BF16)
        row_ref[(count + 1) * BLOCK] = south[1].astype(BF16)
    fill_sides(side_s, west_ref[...], east_ref[...], side_metric_ref, coef_s, north, south)

    def turn(g):
        for r in range(BLOCK):
            row = x_ref[g * BLOCK + r].T
            yield
            row_ref[(g + 1) * BLOCK + r] = row
            yield

    def stencil(g):
        def write(r, normed):
            normed_ref[g * BLOCK + r] = normed

        yield from stencil_block(
            g, lambda q, cs: row_ref[q + BLOCK, cs, :], metric_ref, side_s, coef_s, vec_s, acc_s, lane, write
        )

    def copy(g, carry):
        for r in range(BLOCK):
            row_ref[(g + 1) * BLOCK + r] = old_row_ref[(g + 1) * BLOCK + r]
            normed_ref[g * BLOCK + r] = old_normed_ref[g * BLOCK + r]
        return carry

    def span(lo, hi):
        low, high = max(lo - 1, 0), min(hi + 1, count)
        stages = {"T": (turn, 0, low, high), "S": (stencil, 2, lo, hi)}
        run_stages(stages, (("T", 0),), low, lo + 2, True)
        full = min(high, hi + 2)
        run_stages(stages, ORDER_ONE, lo + 2, full, False)
        run_stages(stages, (("S", 0),), full, hi + 2, True)

    if before:
        lax.fori_loop(1, 1 + before, copy, 0)
    if wrap:
        span(0, 1)
    span(begin, end)


def second_kernel(normed_ref, row_ref, metric_ref, side_metric_ref, lines_ref, sides_ref, coef_ref, gain_ref, bias_ref, w_ref,
                  out_hbm, out_ref, state_s, side_s, acc_s, rows_s, coef_s, vec_s, old_vec_s, m0_s, wg_s,
                  msg1_s, msg2_s, normed_s, flip_s, south_s, sem):
    count = out_ref.shape[0] // BLOCK
    lane = lax.broadcasted_iota(jnp.int32, (8, LANES), 1)
    load_vectors(0, coef_ref, gain_ref, bias_ref, rows_s, coef_s, old_vec_s)
    load_vectors(1, coef_ref, gain_ref, bias_ref, rows_s, coef_s, vec_s)
    for it in range(2):
        load_weights(it, w_ref, m0_s.at[it], wg_s.at[it])
    north, south = turned_lines(lines_ref[0]), turned_lines(lines_ref[1])
    state_s[2 * DEPTH - 1] = north[1].astype(BF16)
    south_s[...] = south[1].astype(BF16)
    fill_sides(side_s, sides_ref[0], sides_ref[1], side_metric_ref, coef_s, north, south)

    def message_one(g):
        buf = lax.rem(g, 2)
        normed = jnp.concatenate([normed_ref[g * BLOCK + r] for r in range(BLOCK)], axis=1)

        def write(ls, value):
            msg1_s[buf, :, ls] = value

        yield from message_block(normed, m0_s.at[0], old_vec_s, write)

    def gates_one(g):
        buf = lax.rem(g, 2)

        def write(r, cs, value):
            state_s[lax.rem(g * BLOCK + r, 2 * DEPTH), cs, :] = value

        yield from gates_block(lambda ls: msg1_s[buf, :, ls], lambda r, cs: row_ref[(g + 1) * BLOCK + r, cs, :], wg_s.at[0], old_vec_s, write)

    def stencil(g):
        buf = lax.rem(g, 2)

        def write(r, normed):
            normed_s[buf, :, LANES * r : LANES * r + LANES] = normed

        def part(q, cs):
            return state_s[lax.rem(q + 2 * DEPTH, 2 * DEPTH), cs, :]

        yield from stencil_block(g, part, metric_ref, side_s, coef_s, vec_s, acc_s, lane, write)

    def message_two(g):
        buf = lax.rem(g, 2)

        def write(ls, value):
            msg2_s[buf, :, ls] = value

        yield from message_block(normed_s[buf], m0_s.at[1], vec_s, write)

    def gates_two(g):
        buf = lax.rem(g, 2)

        def write(r, cs, value):
            flip_s[r, cs, :] = value

        yield from gates_block(
            lambda ls: msg2_s[buf, :, ls],
            lambda r, cs: state_s[lax.rem(g * BLOCK + r, 2 * DEPTH), cs, :],
            wg_s.at[1],
            vec_s,
            write,
        )
        for r in range(BLOCK):
            out_ref[g * BLOCK + r] = flip_s[r].T

    def store(g):
        at = pl.ds(g * BLOCK, BLOCK)
        pltpu.make_async_copy(out_ref.at[at], out_hbm.at[at], sem).start()
        yield

    stages = {
        "m": (message_one, 0, 0, count),
        "g": (gates_one, 1, 0, count),
        "S": (stencil, 3, 0, count),
        "M": (message_two, 4, 0, count),
        "G": (gates_two, 5, 0, count),
        "O": (store, 5, 0, count),
    }
    run_stages(stages, ORDER_TWO, 0, 5, True)
    run_stages(stages, ORDER_TWO, 5, count, False)
    state_s[(count * BLOCK) % (2 * DEPTH)] = south_s[...]
    run_stages(stages, ORDER_TWO, count, count + 5, True)
    pltpu.make_async_copy(out_ref, out_hbm, sem).wait()


def fetch_kernel(state_hbm, metric_hbm, state_ref, metric_ref, sems):
    part = state_ref.shape[0] // 8
    copies = [pltpu.make_async_copy(metric_hbm, metric_ref, sems.at[8])]
    for n in range(8):
        at = pl.ds(n * part, part)
        copies.append(pltpu.make_async_copy(state_hbm.at[at], state_ref.at[at], sems.at[n]))
    for copy in copies:
        copy.start()
    for copy in copies:
        copy.wait()
    for a in range(3):
        metric_ref[3 * a] = pltpu.roll(metric_ref[3 * a], LANES - 1, 1)
        metric_ref[3 * a + 2] = pltpu.roll(metric_ref[3 * a + 2], 1, 1)


def edge_kernel(flags_ref, state_hbm, metric_hbm, near_ref, far_ref, rows_ref, sides_ref, west_s, east_s, metric_ref,
                strip_s, line_s, sems):
    rows, cols = state_hbm.shape[0], state_hbm.shape[1]
    copies = [
        pltpu.make_async_copy(state_hbm.at[:, 0:16, :], west_s, sems.at[0]),
        pltpu.make_async_copy(state_hbm.at[:, cols - 16 : cols, :], east_s, sems.at[1]),
        pltpu.make_async_copy(metric_hbm, metric_ref, sems.at[2]),
    ]
    for copy in copies:
        copy.start()
    for copy in copies:
        copy.wait()
    east_near = flags_ref[0] == 1
    out = lax.broadcasted_iota(jnp.int32, (32, 256), 0)
    source = lax.broadcasted_iota(jnp.int32, (32, 256), 1)

    def picker(first):
        return jnp.where(source == (out % 16) * 16 + first + out // 16, 1.0, 0.0).astype(BF16)

    pick_w, pick_e = picker(0), picker(14)
    for part in range(rows // 16):
        at = slice(16 * part, 16 * part + 16)
        west = west_s[at].reshape(256, LANES)
        east = east_s[at].reshape(256, LANES)
        west = jnp.dot(pick_w, west, preferred_element_type=F32)
        east = jnp.dot(pick_e, east, preferred_element_type=F32)
        near = jnp.where(east_near, east, west).astype(BF16)
        far = jnp.where(east_near, west, east).astype(BF16)
        for n in range(2):
            to = n * rows + 16 * part
            near_ref[to : to + 16, :] = near[16 * n : 16 * n + 16]
            far_ref[to : to + 16, :] = far[16 * n : 16 * n + 16]
    line_s[...] = jnp.zeros_like(line_s)
    for d in range(9):
        upright = metric_ref[d].T
        line_s[0, d : d + 1, :] = upright[0:1]
        line_s[1, d : d + 1, :] = upright[LANES - 1 : LANES]
        line_s[2, d : d + 1, :] = metric_ref[d, 0:1, :]
        line_s[3, d : d + 1, :] = metric_ref[d, rows - 1 : rows, :]
    for n in range(4):
        high = line_s[n].astype(BF16)
        strip_s[n, 0:16, :] = high
        strip_s[n, 16:32, :] = (line_s[n] - high.astype(F32)).astype(BF16)
    west, east = strip_s[0].astype(F32), strip_s[1].astype(F32)
    near_ref[2 * rows : 2 * rows + 32, :] = jnp.where(east_near, east, west).astype(BF16)
    far_ref[2 * rows : 2 * rows + 32, :] = jnp.where(east_near, west, east).astype(BF16)
    sides_ref[...] = line_s[0:2]
    rows_ref[0] = strip_s[2]
    rows_ref[1] = strip_s[3]


def ring_kernel(flags_ref, north_ref, south_ref, west_ref, east_ref, own_rows_ref, own_cols_ref,
                row_metric_ref, col_metric_ref, coef_ref, gain_ref, bias_ref, w_ref,
                lines_ref, sides_ref, line_s, metric_s, new_s):
    polar = [flags_ref[1] == 1, flags_ref[2] == 1]
    ghost = [north_ref, south_ref]
    side = [west_ref, east_ref]

    def put(strip, n, value):
        line_s[strip, n, 8 : 8 + LINE, :] = value

    for e in range(2):
        outer = ghost[e][1].astype(F32)
        inner = own_rows_ref[e].astype(F32)
        before, after = (outer, inner) if e == 0 else (inner, outer)
        put(e, 0, jnp.where(polar[e], after, before))
        put(e, 1, ghost[e][0].astype(F32))
        put(e, 2, jnp.where(polar[e], before, after))
    for e in range(2):
        columns = [side[e][0], side[e][1], own_cols_ref[e]] if e == 0 else [side[e][1], side[e][0], own_cols_ref[e]]
        if e == 1:
            columns = columns[::-1]
        for n in range(3):
            at = n if e == 0 else 129 + n
            line_s[2 + e, n, 0:8, :] = jnp.zeros((8, LANES), F32)
            line_s[2 + e, n, 136:152, :] = jnp.zeros((16, LANES), F32)
            line_s[2 + e, n, 10:138, :] = columns[n].astype(F32)
            line_s[2 + e, n, 9:10, :] = line_s[0, 1, 8 + at : 9 + at, :]
            line_s[2 + e, n, 138:139, :] = line_s[1, 1, 8 + at : 9 + at, :]

    def upright(packed):
        both = packed.astype(F32)
        tall = jnp.concatenate([both[0:16] + both[16:32], jnp.zeros((LANES - 16, LANES), F32)], axis=0)
        return tall.T

    metric_s[...] = jnp.zeros_like(metric_s)
    for e in range(2):
        metric_s[e, 2:130, :] = upright(row_metric_ref[e, 0:32])
        ends = upright(row_metric_ref[e, 32:64])
        metric_s[e, 1:2, :] = ends[0:1]
        metric_s[e, 130:131, :] = ends[1:2]
        metric_s[2 + e, 2:130, :] = upright(col_metric_ref[e])
    normed = []
    old = []
    for strip in range(4):
        metric = metric_s[strip]
        total = None
        for n in range(3):
            for shift in range(3):
                d = 3 * n + shift if strip < 2 else 3 * shift + n
                cells = line_s[strip, n, 7 + shift : 7 + shift + LINE, :]
                term = metric[:, d : d + 1] * coef_ref[d, 0:1, :] * cells
                total = term if total is None else total + term
        scale = lax.rsqrt(jnp.mean(total * total, axis=1, keepdims=True) + EPSILON)
        normed.append(total * scale * gain_ref[0:1, :])
        old.append(line_s[strip, 1, 8 : 8 + LINE, :])
    normed = jnp.concatenate(normed, 0).astype(BF16)
    old = jnp.concatenate(old, 0)

    def mat(k):
        return w_ref[0, k * LANES : (k + 1) * LANES, :]

    def dot(a, k):
        return jnp.dot(a, mat(k), preferred_element_type=F32)

    message = (dot(normed, 0) + bias_ref[0, 0:1, :]).astype(BF16)
    hidden = old.astype(BF16)
    update = 0.5 * jnp.tanh(0.5 * (dot(message, 1) + dot(hidden, 4) + bias_ref[0, 1:2, :])) + 0.5
    reset = 0.5 * jnp.tanh(0.5 * (dot(message, 2) + dot(hidden, 5) + bias_ref[0, 2:3, :])) + 0.5
    new = jnp.tanh(dot(message, 3) + bias_ref[0, 3:4, :] + reset * dot(hidden, 6))
    new_s[...] = (1.0 - update) * new + update * old
    for e in range(2):
        lines_ref[e] = new_s[e * LINE : (e + 1) * LINE, :].astype(BF16)
        sides_ref[e] = new_s[(2 + e) * LINE + 2 : (2 + e) * LINE + 130, :].astype(BF16)


def call(kernel, name, outs, scratch, args, smem=0, hbm=0, far_out=False, flops=0, traffic=0, limit=24):
    vmem = pl.BlockSpec(memory_space=pltpu.VMEM)
    scalar = pl.BlockSpec(memory_space=pltpu.SMEM)
    far = pl.BlockSpec(memory_space=pltpu.HBM)
    return pl.pallas_call(
        kernel,
        in_specs=[scalar] * smem + [far] * hbm + [vmem] * (len(args) - smem - hbm),
        out_specs=[far if far_out else vmem] * len(outs),
        out_shape=[s if hasattr(s, "dtype") else jax.ShapeDtypeStruct(s, BF16) for s in outs],
        scratch_shapes=scratch,
        compiler_params=pltpu.CompilerParams(vmem_limit_bytes=limit * 1024 * 1024),
        cost_estimate=pl.CostEstimate(flops=flops, bytes_accessed=traffic, transcendentals=0),
        name=name,
    )(*args)


def swap(mesh_shape, partner, value):
    lat, lon = mesh_shape
    pairs = [(i * lon + k, partner(i, k)[0] * lon + partner(i, k)[1]) for i in range(lat) for k in range(lon)]
    return lax.ppermute(value, ("lat", "lon"), pairs)


def on_device(state, edge_metric, stencil_coef, norm_gain, biases, weights):
    lat, lon = lax.axis_size("lat"), lax.axis_size("lon")
    shape = (lat, lon)
    half = lon // 2
    i, k = lax.axis_index("lat"), lax.axis_index("lon")
    rows, cols, channels = state.shape
    k_even = k % 2 == 0
    i_even = i % 2 == 0

    def ordered(first, mine, theirs):
        return jnp.where(first, jnp.concatenate([mine, theirs]), jnp.concatenate([theirs, mine]))

    def halves(first, a, b):
        return jnp.where(first, a, b), jnp.where(first, b, a)

    def after(value, *others):
        return lax.optimization_barrier((value,) + others)[0]

    shard = weights.transpose(1, 0, 2).reshape(-1, channels)
    stencil_coef = stencil_coef.transpose(1, 0, 2)

    vmem = pltpu.VMEM
    flags = jnp.stack([k_even, i == 0, i == lat - 1]).astype(jnp.int32)
    size = 2 * rows + 32
    near, far, row_metrics, side_metric = call(
        edge_kernel,
        "edges",
        [(size, channels), (size, channels), (2, 32, cols), jax.ShapeDtypeStruct((2, 16, rows), F32)],
        [
            vmem((rows, 16, channels), BF16),
            vmem((rows, 16, channels), BF16),
            vmem(edge_metric.shape, F32),
            vmem((4, 32, LANES), BF16),
            vmem((4, 16, LANES), F32),
            pltpu.SemaphoreType.DMA((3,)),
        ],
        (flags, state, edge_metric),
        smem=1,
        hbm=2,
        limit=12,
    )
    got_near = swap(shape, lambda i, k: (i, k ^ 1), jnp.concatenate([near, shard]))
    size = 2 * rows + 32
    shard = ordered(k_even, shard, got_near[size:])
    far_shard = jnp.concatenate([far, shard])
    got_far = swap(shape, lambda i, k: (i, (k + 1) % lon if k % 2 else (k - 1) % lon), far_shard)
    near_state, near_metric = call(
        fetch_kernel,
        "fetch",
        [state, edge_metric],
        [pltpu.SemaphoreType.DMA((9,))],
        (after(state, far_shard), edge_metric),
        hbm=2,
        traffic=8 * state.size,
        limit=12,
    )
    shard = ordered(jnp.logical_not(k_even), shard, got_far[size:])
    in_e, in_w = halves(k_even, got_near[:size], got_far[:size])
    ghost_w, ghost_e = (a[: 2 * rows].reshape(2, rows, channels) for a in (in_w, in_e))
    metric_w, metric_e = in_w[2 * rows :], in_e[2 * rows :]
    own_e, own_w = halves(k_even, near, far)

    def extended(row, inner):
        lines = []
        for q in (row, inner):
            fill = jnp.zeros((LINE - cols - 4, channels), BF16)
            lines.append(jnp.concatenate([ghost_w[:, q], near_state[q], ghost_e[:, q], fill]))
        return jnp.stack(lines)

    def extended_metric(row, body):
        ends = jnp.concatenate([metric_w[:, row : row + 1], metric_e[:, row : row + 1]], axis=1)
        ends = jnp.pad(ends, ((0, 0), (0, LANES - 2)))
        return jnp.concatenate([body, ends])

    row_n, row_s = extended(0, 1), extended(rows - 1, rows - 2)
    out_n = jnp.concatenate([row_n.reshape(-1, channels), extended_metric(0, row_metrics[0])])
    out_s = jnp.concatenate([row_s.reshape(-1, channels), extended_metric(rows - 1, row_metrics[1])])
    size = out_n.shape[0]
    send_a, send_b = halves(i_even, out_s, out_n)
    send_a = jnp.concatenate([send_a, shard])

    def across(i, k):
        if i == 0 or i == lat - 1:
            return i, (k + half) % lon
        return (i + 1, k) if i % 2 else (i - 1, k)

    got_a = swap(shape, lambda i, k: (i ^ 1, k), send_a)
    got_b = swap(shape, across, send_b)

    tile = state.shape
    square = (LANES, LANES)
    count = rows // BLOCK
    cuts = [1, 1 + (count - 1) // 3, 1 + 2 * (count - 1) // 3, count]

    def aggregate(part, side_w, more):
        begin, end = cuts[part], cuts[part + 1]
        return call(
            functools.partial(first_kernel, begin, end, begin - 1, part == 2),
            "aggregate%d" % part,
            [(rows + 2 * BLOCK,) + square, tile],
            [
                vmem((2,) + square, F32),
                vmem((LANES, 2 * LANES), F32),
                vmem(square, F32),
                vmem((9,) + square, F32),
                vmem((5,) + square, F32),
            ],
            (near_state, near_metric, side_metric, side_w, ghost_e[0], stencil_coef, norm_gain, biases) + more,
            flops=20 * state.size,
            traffic=8 * state.size,
        )

    held = aggregate(0, after(ghost_w[1], send_a, send_b), ())

    shard = ordered((i & 1) == 0, shard, got_a[size:])
    in_s, in_n = halves(i_even, got_a[:size], got_b)
    ghost_n, ghost_s = (a[: 2 * LINE].reshape(2, LINE, channels) for a in (in_n, in_s))
    row_metric = jnp.stack([in_n[2 * LINE :], in_s[2 * LINE :]])

    shard = shard.reshape(2, 4, -1, channels)
    bit = 4
    while bit < lon:
        mine = after(shard, *held) if bit == 4 else shard
        got = swap(shape, lambda i, k, bit=bit: (i, k ^ bit), mine)
        low = (k & bit) == 0
        shard = jnp.where(
            low, jnp.concatenate([shard, got], axis=1), jnp.concatenate([got, shard], axis=1)
        )
        if bit == 4:
            held = aggregate(1, after(ghost_w[1], mine), tuple(held))
        bit *= 2
    place = k % 4
    shard = jnp.where(
        place == 0,
        jnp.roll(shard, -2, axis=1),
        jnp.where(place == 3, jnp.roll(shard, 2, axis=1), shard),
    )
    shard = shard.reshape(-1, channels)
    bit = 2
    while bit < lat:
        mine = after(shard, *held) if bit == 2 else shard
        got = swap(shape, lambda i, k, bit=bit: (i ^ bit, k), mine)
        shard = ordered((i & bit) == 0, shard, got)
        if bit == 2:
            held = aggregate(2, after(ghost_w[1], mine), (ghost_n[0], ghost_s[0]) + tuple(held))
        bit *= 2
    row_t, normed = held
    full = shard.reshape(-1, ITERS, channels).transpose(1, 0, 2)

    lines, sides = call(
        ring_kernel,
        "border",
        [(2, LINE, channels), (2, rows, channels)],
        [vmem((4, 3, LINE + 16, LANES), F32), vmem((4, LINE, LANES), F32), vmem((4 * LINE, LANES), F32)],
        (
            flags,
            ghost_n,
            ghost_s,
            ghost_w,
            ghost_e,
            jnp.stack([row_n[0], row_s[0]]),
            jnp.stack([own_w[:rows], own_e[rows : 2 * rows]]),
            row_metric,
            jnp.stack([metric_w, metric_e]),
            stencil_coef,
            norm_gain,
            biases,
            full,
        ),
        smem=1,
        limit=12,
    )
    (out,) = call(
        second_kernel,
        "refine",
        [tile],
        [
            vmem(tile, BF16),
            vmem((2 * DEPTH,) + square, BF16),
            vmem((2,) + square, F32),
            vmem((LANES, 2 * LANES), F32),
            vmem(square, F32),
            vmem((9,) + square, F32),
            vmem((5,) + square, F32),
            vmem((5,) + square, F32),
            vmem((2,) + square, BF16),
            vmem((2, 4 * LANES, 2 * LANES), BF16),
            vmem((2, LANES, BLOCK * LANES), BF16),
            vmem((2, LANES, BLOCK * LANES), BF16),
            vmem((2, LANES, BLOCK * LANES), BF16),
            vmem((BLOCK,) + square, BF16),
            vmem(square, BF16),
            pltpu.SemaphoreType.DMA,
        ],
        (normed, row_t, near_metric, side_metric, lines, sides, stencil_coef, norm_gain, biases, full),
        far_out=True,
    )
    return out


def solution(mesh):
    in_specs = (
        P("lat", "lon", None),
        P(None, "lat", "lon"),
        P(),
        P(),
        P(),
        P(None, ("lat", "lon"), None),
    )
    out_specs = P("lat", "lon", None)
    return jax.shard_map(on_device, mesh=mesh, in_specs=in_specs, out_specs=out_specs, check_vma=False)
```

```python
import functools

import jax
import jax.numpy as jnp
from jax import lax
from jax.experimental import pallas as pl
from jax.experimental.pallas import tpu as pltpu
from jax.sharding import PartitionSpec as P

KMAT = 7
ITERS = 2
EPSILON = 1e-05
LANES = 128
BLOCK = 4
DEPTH = 4 * BLOCK
LINE = 136
ORDER_ONE = (("S", 0), ("T", 0))
ORDER_TWO = (("G", 99), ("M", 99), ("S", 99), ("g", 99), ("m", 99), ("O", 99))
F32 = jnp.float32
BF16 = jnp.bfloat16


def twice(a):
    return jnp.concatenate([a, a], axis=1)


def load_vectors(it, coef_ref, gain_ref, bias_ref, rows_s, coef_s, vec_s):
    rows_s[...] = jnp.zeros_like(rows_s)
    rows_s[0:9, :] = coef_ref[:, it, :]
    rows_s[9:10, :] = gain_ref[it : it + 1, :]
    rows_s[10:14, :] = bias_ref[it]
    columns = rows_s[...].T
    for d in range(9):
        coef_s[d] = jnp.broadcast_to(columns[:, d : d + 1], (LANES, LANES))
    for k in range(5):
        factor = 0.5 if k in (2, 3) else 1.0
        vec_s[k] = jnp.broadcast_to(columns[:, 9 + k : 10 + k] * factor, (LANES, LANES))


def load_weights(it, w_ref, m0_s, wg_s):
    def mat(k):
        return w_ref[it, k * LANES : (k + 1) * LANES, :].astype(F32).T

    m0_s[...] = mat(0).astype(BF16)
    h1, h2, h4, h5, h6 = (mat(k) * 0.5 for k in (1, 2, 4, 5, 6))
    parts = [
        jnp.concatenate([h1, h4], 1),
        jnp.concatenate([h2, h5], 1),
        jnp.concatenate([mat(3), h6], 1),
        jnp.concatenate([jnp.zeros_like(h6), h6], 1),
    ]
    for g in range(8):
        for n, part in enumerate(parts):
            wg_s[64 * g + 16 * n : 64 * g + 16 * n + 16, :] = part[16 * g : 16 * g + 16].astype(BF16)


def turned_lines(line):
    wide = line.astype(F32)
    return [wide[1 + b : 129 + b].T for b in range(3)]


def fill_sides(side_s, west, east, side_metric_ref, coef_s, north, south):
    lane = lax.broadcasted_iota(jnp.int32, (LANES, LANES), 1)

    def part(side, column, above, below):
        middle = side.astype(F32).T
        upper, lower = pltpu.roll(middle, 1, 1), pltpu.roll(middle, LANES - 1, 1)
        if above is not None:
            upper = jnp.where(lane == 0, above, upper)
            lower = jnp.where(lane == LANES - 1, below, lower)
        total = None
        for a, cells in enumerate((upper, middle, lower)):
            d = 3 * a + 2 * column
            term = (cells * coef_s[d]) * side_metric_ref[column, d : d + 1, :]
            total = term if total is None else total + term
        return total

    ends = [None] * 4
    if north is not None:
        ends = [north[0][:, 0:1], south[0][:, 0:1], north[2][:, LANES - 1 :], south[2][:, LANES - 1 :]]
    first = part(west, 0, ends[0], ends[1])
    last = pltpu.roll(part(east, 1, ends[2], ends[3]), LANES - 1, 1)
    odd = lane % 2 == 1
    side_s[0] = jnp.where(odd, last, first)
    side_s[1] = jnp.where(odd, first, last)


def stencil_block(g, read_part, metric_ref, side_s, coef_s, vec_s, acc_s, lane, write):
    for pair in range(BLOCK // 2):
        first = g * BLOCK + 2 * pair
        squares = [None, None]
        turns = [lax.rem(2 * LANES - first - r, LANES) for r in range(2)]
        metric = [
            [jnp.broadcast_to(metric_ref[d, pl.ds(first + r, 1), :], (8, LANES)) for r in range(2)]
            for d in range(9)
        ]
        for group in range(LANES // 16):
            rows = [read_part(first - 1 + k, slice(16 * group, 16 * group + 16)).astype(F32) for k in range(4)]
            for half in range(2):
                cs = slice(16 * group + 8 * half, 16 * group + 8 * half + 8)
                cells = [row[8 * half : 8 * half + 8] for row in rows]
                for r in range(2):
                    sums = []
                    for b in range(3):
                        total = None
                        for a in range(3):
                            d = 3 * a + b
                            term = (cells[r + a] * coef_s[d, cs, :]) * metric[d][r]
                            total = term if total is None else total + term
                        sums.append(total)
                    side = pltpu.roll(side_s[r, cs, :], turns[r], 1)
                    west = jnp.where(lane == 0, side, pltpu.roll(sums[0], 1, 1))
                    east = jnp.where(lane == LANES - 1, side, pltpu.roll(sums[2], LANES - 1, 1))
                    total = (sums[1] + west) + east
                    square = total * total
                    squares[r] = square if squares[r] is None else squares[r] + square
                    acc_s[cs, LANES * r : LANES * r + LANES] = total
                yield
        for r in range(2):
            mean = jnp.sum(squares[r], axis=0, keepdims=True) * (1.0 / LANES)
            scale = lax.rsqrt(mean + EPSILON)
            total = acc_s[:, LANES * r : LANES * r + LANES]
            write(2 * pair + r, (total * scale * vec_s[0]).astype(BF16))


def message_block(normed, m0_s, vec_s, write):
    product = jnp.dot(m0_s[...], normed, preferred_element_type=F32)
    yield
    for pair in range(BLOCK // 2):
        ls = slice(2 * LANES * pair, 2 * LANES * (pair + 1))
        write(ls, (product[:, ls] + twice(vec_s[1])).astype(BF16))
        yield


def gates_block(read_message, read_part, wg_s, vec_s, write):
    products = []
    for pair in range(BLOCK // 2):
        ls = slice(2 * LANES * pair, 2 * LANES * (pair + 1))
        whole = slice(0, LANES)
        current = jnp.concatenate([read_part(2 * pair, whole), read_part(2 * pair + 1, whole)], axis=1)
        both = jnp.concatenate([read_message(ls), current], axis=0)
        products.append(jnp.dot(wg_s[...], both, preferred_element_type=F32))
    yield
    for pair in range(BLOCK // 2):
        w = products[pair]
        for g in range(8):
            o = 64 * g
            cs = slice(16 * g, 16 * g + 16)
            old = jnp.concatenate([read_part(2 * pair, cs), read_part(2 * pair + 1, cs)], axis=1).astype(F32)
            update = jnp.tanh(w[o : o + 16] + twice(vec_s[2, cs, :]))
            reset = jnp.tanh(w[o + 16 : o + 32] + twice(vec_s[3, cs, :]))
            inner = (w[o + 32 : o + 48] + twice(vec_s[4, cs, :])) + reset * w[o + 48 : o + 64]
            new = jnp.tanh(inner)
            blend = ((old + new) + update * (old - new)) * 0.5
            blend = blend.astype(BF16)
            for r in range(2):
                write(2 * pair + r, cs, blend[:, LANES * r : LANES * r + LANES])
            yield


def run_stages(stages, order, first, last, guarded):
    names = list(dict.fromkeys(name for name, _ in order))

    def step(s, carry, valid=None):
        here = [name for name in names if valid is None or valid(name)]
        parts = {name: stages[name][0](s - stages[name][1]) for name in here}
        for name, pieces in order:
            for _ in range(pieces if name in here else 0):
                next(parts[name], None)
        for name in here:
            for _ in parts[name]:
                pass
        return carry

    if guarded:
        for s in range(first, last):
            step(s, 0, lambda name: stages[name][2] <= s - stages[name][1] < stages[name][3])
    else:
        lax.fori_loop(first, last, step, 0)


def first_kernel(begin, end, before, wrap, *refs):
    x_ref, metric_ref, side_metric_ref, west_ref, east_ref, coef_ref, gain_ref, bias_ref = refs[:8]
    rest = refs[8:]
    if wrap:
        north_ref, south_ref = rest[:2]
        rest = rest[2:]
    if before:
        old_row_ref, old_normed_ref = rest[:2]
        rest = rest[2:]
    row_ref, normed_ref, side_s, acc_s, rows_s, coef_s, vec_s = rest
    lane = lax.broadcasted_iota(jnp.int32, (8, LANES), 1)
    count = x_ref.shape[0] // BLOCK
    load_vectors(0, coef_ref, gain_ref, bias_ref, rows_s, coef_s, vec_s)
    north = south = None
    if wrap:
        north, south = turned_lines(north_ref[...]), turned_lines(south_ref[...])
        row_ref[BLOCK - 1] = north[1].astype(BF16)
        row_ref[(count + 1) * BLOCK] = south[1].astype(BF16)
    fill_sides(side_s, west_ref[...], east_ref[...], side_metric_ref, coef_s, north, south)

    def turn(g):
        for r in range(BLOCK):
            row = x_ref[g * BLOCK + r].T
            yield
            row_ref[(g + 1) * BLOCK + r] = row
            yield

    def stencil(g):
        def write(r, normed):
            normed_ref[g * BLOCK + r] = normed

        yield from stencil_block(
            g, lambda q, cs: row_ref[q + BLOCK, cs, :], metric_ref, side_s, coef_s, vec_s, acc_s, lane, write
        )

    def copy(g, carry):
        for r in range(BLOCK):
            row_ref[(g + 1) * BLOCK + r] = old_row_ref[(g + 1) * BLOCK + r]
            normed_ref[g * BLOCK + r] = old_normed_ref[g * BLOCK + r]
        return carry

    def span(lo, hi):
        low, high = max(lo - 1, 0), min(hi + 1, count)
        stages = {"T": (turn, 0, low, high), "S": (stencil, 2, lo, hi)}
        run_stages(stages, (("T", 0),), low, lo + 2, True)
        full = min(high, hi + 2)
        run_stages(stages, ORDER_ONE, lo + 2, full, False)
        run_stages(stages, (("S", 0),), full, hi + 2, True)

    if before:
        lax.fori_loop(1, 1 + before, copy, 0)
    if wrap:
        span(0, 1)
    span(begin, end)


def second_kernel(normed_ref, row_ref, metric_ref, side_metric_ref, lines_ref, sides_ref, coef_ref, gain_ref, bias_ref, w_ref,
                  out_hbm, out_ref, state_s, side_s, acc_s, rows_s, coef_s, vec_s, old_vec_s, m0_s, wg_s,
                  msg1_s, msg2_s, normed_s, flip_s, south_s, sem):
    count = out_ref.shape[0] // BLOCK
    lane = lax.broadcasted_iota(jnp.int32, (8, LANES), 1)
    load_vectors(0, coef_ref, gain_ref, bias_ref, rows_s, coef_s, old_vec_s)
    load_vectors(1, coef_ref, gain_ref, bias_ref, rows_s, coef_s, vec_s)
    for it in range(2):
        load_weights(it, w_ref, m0_s.at[it], wg_s.at[it])
    north, south = turned_lines(lines_ref[0]), turned_lines(lines_ref[1])
    state_s[2 * DEPTH - 1] = north[1].astype(BF16)
    south_s[...] = south[1].astype(BF16)
    fill_sides(side_s, sides_ref[0], sides_ref[1], side_metric_ref, coef_s, north, south)

    def message_one(g):
        buf = lax.rem(g, 2)
        normed = jnp.concatenate([normed_ref[g * BLOCK + r] for r in range(BLOCK)], axis=1)

        def write(ls, value):
            msg1_s[buf, :, ls] = value

        yield from message_block(normed, m0_s.at[0], old_vec_s, write)

    def gates_one(g):
        buf = lax.rem(g, 2)

        def write(r, cs, value):
            state_s[lax.rem(g * BLOCK + r, 2 * DEPTH), cs, :] = value

        yield from gates_block(lambda ls: msg1_s[buf, :, ls], lambda r, cs: row_ref[(g + 1) * BLOCK + r, cs, :], wg_s.at[0], old_vec_s, write)

    def stencil(g):
        buf = lax.rem(g, 2)

        def write(r, normed):
            normed_s[buf, :, LANES * r : LANES * r + LANES] = normed

        def part(q, cs):
            return state_s[lax.rem(q + 2 * DEPTH, 2 * DEPTH), cs, :]

        yield from stencil_block(g, part, metric_ref, side_s, coef_s, vec_s, acc_s, lane, write)

    def message_two(g):
        buf = lax.rem(g, 2)

        def write(ls, value):
            msg2_s[buf, :, ls] = value

        yield from message_block(normed_s[buf], m0_s.at[1], vec_s, write)

    def gates_two(g):
        buf = lax.rem(g, 2)

        def write(r, cs, value):
            flip_s[r, cs, :] = value

        yield from gates_block(
            lambda ls: msg2_s[buf, :, ls],
            lambda r, cs: state_s[lax.rem(g * BLOCK + r, 2 * DEPTH), cs, :],
            wg_s.at[1],
            vec_s,
            write,
        )
        for r in range(BLOCK):
            out_ref[g * BLOCK + r] = flip_s[r].T

    def store(g):
        at = pl.ds(g * BLOCK, BLOCK)
        pltpu.make_async_copy(out_ref.at[at], out_hbm.at[at], sem).start()
        yield

    stages = {
        "m": (message_one, 0, 0, count),
        "g": (gates_one, 1, 0, count),
        "S": (stencil, 3, 0, count),
        "M": (message_two, 4, 0, count),
        "G": (gates_two, 5, 0, count),
        "O": (store, 5, 0, count),
    }
    run_stages(stages, ORDER_TWO, 0, 5, True)
    run_stages(stages, ORDER_TWO, 5, count, False)
    state_s[(count * BLOCK) % (2 * DEPTH)] = south_s[...]
    run_stages(stages, ORDER_TWO, count, count + 5, True)
    pltpu.make_async_copy(out_ref, out_hbm, sem).wait()


def fetch_kernel(state_hbm, metric_hbm, state_ref, metric_ref, sems):
    part = state_ref.shape[0] // 8
    copies = [pltpu.make_async_copy(metric_hbm, metric_ref, sems.at[8])]
    for n in range(8):
        at = pl.ds(n * part, part)
        copies.append(pltpu.make_async_copy(state_hbm.at[at], state_ref.at[at], sems.at[n]))
    for copy in copies:
        copy.start()
    for copy in copies:
        copy.wait()
    for a in range(3):
        metric_ref[3 * a] = pltpu.roll(metric_ref[3 * a], LANES - 1, 1)
        metric_ref[3 * a + 2] = pltpu.roll(metric_ref[3 * a + 2], 1, 1)


def edge_kernel(flags_ref, state_hbm, metric_hbm, near_ref, far_ref, rows_ref, sides_ref, west_s, east_s, metric_ref,
                strip_s, line_s, sems):
    rows, cols = state_hbm.shape[0], state_hbm.shape[1]
    copies = [
        pltpu.make_async_copy(state_hbm.at[:, 0:16, :], west_s, sems.at[0]),
        pltpu.make_async_copy(state_hbm.at[:, cols - 16 : cols, :], east_s, sems.at[1]),
        pltpu.make_async_copy(metric_hbm, metric_ref, sems.at[2]),
    ]
    for copy in copies:
        copy.start()
    for copy in copies:
        copy.wait()
    east_near = flags_ref[0] == 1
    out = lax.broadcasted_iota(jnp.int32, (32, 256), 0)
    source = lax.broadcasted_iota(jnp.int32, (32, 256), 1)

    def picker(first):
        return jnp.where(source == (out % 16) * 16 + first + out // 16, 1.0, 0.0).astype(BF16)

    pick_w, pick_e = picker(0), picker(14)
    for part in range(rows // 16):
        at = slice(16 * part, 16 * part + 16)
        west = west_s[at].reshape(256, LANES)
        east = east_s[at].reshape(256, LANES)
        west = jnp.dot(pick_w, west, preferred_element_type=F32)
        east = jnp.dot(pick_e, east, preferred_element_type=F32)
        near = jnp.where(east_near, east, west).astype(BF16)
        far = jnp.where(east_near, west, east).astype(BF16)
        for n in range(2):
            to = n * rows + 16 * part
            near_ref[to : to + 16, :] = near[16 * n : 16 * n + 16]
            far_ref[to : to + 16, :] = far[16 * n : 16 * n + 16]
    line_s[...] = jnp.zeros_like(line_s)
    for d in range(9):
        upright = metric_ref[d].T
        line_s[0, d : d + 1, :] = upright[0:1]
        line_s[1, d : d + 1, :] = upright[LANES - 1 : LANES]
        line_s[2, d : d + 1, :] = metric_ref[d, 0:1, :]
        line_s[3, d : d + 1, :] = metric_ref[d, rows - 1 : rows, :]
    for n in range(4):
        high = line_s[n].astype(BF16)
        strip_s[n, 0:16, :] = high
        strip_s[n, 16:32, :] = (line_s[n] - high.astype(F32)).astype(BF16)
    west, east = strip_s[0].astype(F32), strip_s[1].astype(F32)
    near_ref[2 * rows : 2 * rows + 32, :] = jnp.where(east_near, east, west).astype(BF16)
    far_ref[2 * rows : 2 * rows + 32, :] = jnp.where(east_near, west, east).astype(BF16)
    sides_ref[...] = line_s[0:2]
    rows_ref[0] = strip_s[2]
    rows_ref[1] = strip_s[3]


def ring_kernel(flags_ref, north_ref, south_ref, west_ref, east_ref, own_rows_ref, own_cols_ref,
                row_metric_ref, col_metric_ref, coef_ref, gain_ref, bias_ref, w_ref,
                lines_ref, sides_ref, line_s, metric_s, new_s):
    polar = [flags_ref[1] == 1, flags_ref[2] == 1]
    ghost = [north_ref, south_ref]
    side = [west_ref, east_ref]

    def put(strip, n, value):
        line_s[strip, n, 8 : 8 + LINE, :] = value

    for e in range(2):
        outer = ghost[e][1].astype(F32)
        inner = own_rows_ref[e].astype(F32)
        before, after = (outer, inner) if e == 0 else (inner, outer)
        put(e, 0, jnp.where(polar[e], after, before))
        put(e, 1, ghost[e][0].astype(F32))
        put(e, 2, jnp.where(polar[e], before, after))
    for e in range(2):
        columns = [side[e][0], side[e][1], own_cols_ref[e]] if e == 0 else [side[e][1], side[e][0], own_cols_ref[e]]
        if e == 1:
            columns = columns[::-1]
        for n in range(3):
            at = n if e == 0 else 129 + n
            line_s[2 + e, n, 0:8, :] = jnp.zeros((8, LANES), F32)
            line_s[2 + e, n, 136:152, :] = jnp.zeros((16, LANES), F32)
            line_s[2 + e, n, 10:138, :] = columns[n].astype(F32)
            line_s[2 + e, n, 9:10, :] = line_s[0, 1, 8 + at : 9 + at, :]
            line_s[2 + e, n, 138:139, :] = line_s[1, 1, 8 + at : 9 + at, :]

    def upright(packed):
        both = packed.astype(F32)
        tall = jnp.concatenate([both[0:16] + both[16:32], jnp.zeros((LANES - 16, LANES), F32)], axis=0)
        return tall.T

    metric_s[...] = jnp.zeros_like(metric_s)
    for e in range(2):
        metric_s[e, 2:130, :] = upright(row_metric_ref[e, 0:32])
        ends = upright(row_metric_ref[e, 32:64])
        metric_s[e, 1:2, :] = ends[0:1]
        metric_s[e, 130:131, :] = ends[1:2]
        metric_s[2 + e, 2:130, :] = upright(col_metric_ref[e])
    normed = []
    old = []
    for strip in range(4):
        metric = metric_s[strip]
        total = None
        for n in range(3):
            for shift in range(3):
                d = 3 * n + shift if strip < 2 else 3 * shift + n
                cells = line_s[strip, n, 7 + shift : 7 + shift + LINE, :]
                term = metric[:, d : d + 1] * coef_ref[d, 0:1, :] * cells
                total = term if total is None else total + term
        scale = lax.rsqrt(jnp.mean(total * total, axis=1, keepdims=True) + EPSILON)
        normed.append(total * scale * gain_ref[0:1, :])
        old.append(line_s[strip, 1, 8 : 8 + LINE, :])
    normed = jnp.concatenate(normed, 0).astype(BF16)
    old = jnp.concatenate(old, 0)

    def mat(k):
        return w_ref[0, k * LANES : (k + 1) * LANES, :]

    def dot(a, k):
        return jnp.dot(a, mat(k), preferred_element_type=F32)

    message = (dot(normed, 0) + bias_ref[0, 0:1, :]).astype(BF16)
    hidden = old.astype(BF16)
    update = 0.5 * jnp.tanh(0.5 * (dot(message, 1) + dot(hidden, 4) + bias_ref[0, 1:2, :])) + 0.5
    reset = 0.5 * jnp.tanh(0.5 * (dot(message, 2) + dot(hidden, 5) + bias_ref[0, 2:3, :])) + 0.5
    new = jnp.tanh(dot(message, 3) + bias_ref[0, 3:4, :] + reset * dot(hidden, 6))
    new_s[...] = (1.0 - update) * new + update * old
    for e in range(2):
        lines_ref[e] = new_s[e * LINE : (e + 1) * LINE, :].astype(BF16)
        sides_ref[e] = new_s[(2 + e) * LINE + 2 : (2 + e) * LINE + 130, :].astype(BF16)


def call(kernel, name, outs, scratch, args, smem=0, hbm=0, far_out=False, flops=0, traffic=0, limit=24):
    vmem = pl.BlockSpec(memory_space=pltpu.VMEM)
    scalar = pl.BlockSpec(memory_space=pltpu.SMEM)
    far = pl.BlockSpec(memory_space=pltpu.HBM)
    return pl.pallas_call(
        kernel,
        in_specs=[scalar] * smem + [far] * hbm + [vmem] * (len(args) - smem - hbm),
        out_specs=[far if far_out else vmem] * len(outs),
        out_shape=[s if hasattr(s, "dtype") else jax.ShapeDtypeStruct(s, BF16) for s in outs],
        scratch_shapes=scratch,
        compiler_params=pltpu.CompilerParams(vmem_limit_bytes=limit * 1024 * 1024),
        cost_estimate=pl.CostEstimate(flops=flops, bytes_accessed=traffic, transcendentals=0),
        name=name,
    )(*args)


def swap(mesh_shape, partner, value):
    lat, lon = mesh_shape
    pairs = [(i * lon + k, partner(i, k)[0] * lon + partner(i, k)[1]) for i in range(lat) for k in range(lon)]
    return lax.ppermute(value, ("lat", "lon"), pairs)


def on_device(state, edge_metric, stencil_coef, norm_gain, biases, weights):
    lat, lon = lax.axis_size("lat"), lax.axis_size("lon")
    shape = (lat, lon)
    half = lon // 2
    i, k = lax.axis_index("lat"), lax.axis_index("lon")
    rows, cols, channels = state.shape
    k_even = k % 2 == 0
    i_even = i % 2 == 0

    def ordered(first, mine, theirs):
        return jnp.where(first, jnp.concatenate([mine, theirs]), jnp.concatenate([theirs, mine]))

    def halves(first, a, b):
        return jnp.where(first, a, b), jnp.where(first, b, a)

    def after(value, *others):
        return lax.optimization_barrier((value,) + others)[0]

    shard = weights.transpose(1, 0, 2).reshape(-1, channels)
    stencil_coef = stencil_coef.transpose(1, 0, 2)

    vmem = pltpu.VMEM
    flags = jnp.stack([k_even, i == 0, i == lat - 1]).astype(jnp.int32)
    size = 2 * rows + 32
    near, far, row_metrics, side_metric = call(
        edge_kernel,
        "edges",
        [(size, channels), (size, channels), (2, 32, cols), jax.ShapeDtypeStruct((2, 16, rows), F32)],
        [
            vmem((rows, 16, channels), BF16),
            vmem((rows, 16, channels), BF16),
            vmem(edge_metric.shape, F32),
            vmem((4, 32, LANES), BF16),
            vmem((4, 16, LANES), F32),
            pltpu.SemaphoreType.DMA((3,)),
        ],
        (flags, state, edge_metric),
        smem=1,
        hbm=2,
        limit=12,
    )
    got_near = swap(shape, lambda i, k: (i, k ^ 1), jnp.concatenate([near, shard]))
    size = 2 * rows + 32
    shard = ordered(k_even, shard, got_near[size:])
    far_shard = jnp.concatenate([far, shard])
    got_far = swap(shape, lambda i, k: (i, (k + 1) % lon if k % 2 else (k - 1) % lon), far_shard)
    near_state, near_metric = call(
        fetch_kernel,
        "fetch",
        [state, edge_metric],
        [pltpu.SemaphoreType.DMA((9,))],
        (after(state, far_shard), edge_metric),
        hbm=2,
        traffic=8 * state.size,
        limit=12,
    )
    shard = ordered(jnp.logical_not(k_even), shard, got_far[size:])
    in_e, in_w = halves(k_even, got_near[:size], got_far[:size])
    ghost_w, ghost_e = (a[: 2 * rows].reshape(2, rows, channels) for a in (in_w, in_e))
    metric_w, metric_e = in_w[2 * rows :], in_e[2 * rows :]
    own_e, own_w = halves(k_even, near, far)

    def extended(row, inner):
        lines = []
        for q in (row, inner):
            fill = jnp.zeros((LINE - cols - 4, channels), BF16)
            lines.append(jnp.concatenate([ghost_w[:, q], near_state[q], ghost_e[:, q], fill]))
        return jnp.stack(lines)

    def extended_metric(row, body):
        ends = jnp.concatenate([metric_w[:, row : row + 1], metric_e[:, row : row + 1]], axis=1)
        ends = jnp.pad(ends, ((0, 0), (0, LANES - 2)))
        return jnp.concatenate([body, ends])

    row_n, row_s = extended(0, 1), extended(rows - 1, rows - 2)
    out_n = jnp.concatenate([row_n.reshape(-1, channels), extended_metric(0, row_metrics[0])])
    out_s = jnp.concatenate([row_s.reshape(-1, channels), extended_metric(rows - 1, row_metrics[1])])
    size = out_n.shape[0]
    send_a, send_b = halves(i_even, out_s, out_n)
    send_a = jnp.concatenate([send_a, shard])

    def across(i, k):
        if i == 0 or i == lat - 1:
            return i, (k + half) % lon
        return (i + 1, k) if i % 2 else (i - 1, k)

    got_a = swap(shape, lambda i, k: (i ^ 1, k), send_a)
    got_b = swap(shape, across, send_b)

    tile = state.shape
    square = (LANES, LANES)
    count = rows // BLOCK
    cuts = [1, 1 + (count - 1) // 3, 1 + 2 * (count - 1) // 3, count]

    def aggregate(part, side_w, more):
        begin, end = cuts[part], cuts[part + 1]
        return call(
            functools.partial(first_kernel, begin, end, begin - 1, part == 2),
            "aggregate%d" % part,
            [(rows + 2 * BLOCK,) + square, tile],
            [
                vmem((2,) + square, F32),
                vmem((LANES, 2 * LANES), F32),
                vmem(square, F32),
                vmem((9,) + square, F32),
                vmem((5,) + square, F32),
            ],
            (near_state, near_metric, side_metric, side_w, ghost_e[0], stencil_coef, norm_gain, biases) + more,
            flops=20 * state.size,
            traffic=8 * state.size,
        )

    held = aggregate(0, after(ghost_w[1], send_a, send_b), ())

    shard = ordered((i & 1) == 0, shard, got_a[size:])
    in_s, in_n = halves(i_even, got_a[:size], got_b)
    ghost_n, ghost_s = (a[: 2 * LINE].reshape(2, LINE, channels) for a in (in_n, in_s))
    row_metric = jnp.stack([in_n[2 * LINE :], in_s[2 * LINE :]])

    shard = shard.reshape(2, 4, -1, channels)
    bit = 4
    while bit < lon:
        mine = after(shard, *held) if bit == 4 else shard
        got = swap(shape, lambda i, k, bit=bit: (i, k ^ bit), mine)
        low = (k & bit) == 0
        shard = jnp.where(
            low, jnp.concatenate([shard, got], axis=1), jnp.concatenate([got, shard], axis=1)
        )
        if bit == 4:
            held = aggregate(1, after(ghost_w[1], mine), tuple(held))
        bit *= 2
    place = k % 4
    shard = jnp.where(
        place == 0,
        jnp.roll(shard, -2, axis=1),
        jnp.where(place == 3, jnp.roll(shard, 2, axis=1), shard),
    )
    shard = shard.reshape(-1, channels)
    bit = 2
    while bit < lat:
        mine = after(shard, *held) if bit == 2 else shard
        got = swap(shape, lambda i, k, bit=bit: (i ^ bit, k), mine)
        shard = ordered((i & bit) == 0, shard, got)
        if bit == 2:
            held = aggregate(2, after(ghost_w[1], mine), (ghost_n[0], ghost_s[0]) + tuple(held))
        bit *= 2
    row_t, normed = held
    full = shard.reshape(-1, ITERS, channels).transpose(1, 0, 2)

    lines, sides = call(
        ring_kernel,
        "border",
        [(2, LINE, channels), (2, rows, channels)],
        [vmem((4, 3, LINE + 16, LANES), F32), vmem((4, LINE, LANES), F32), vmem((4 * LINE, LANES), F32)],
        (
            flags,
            ghost_n,
            ghost_s,
            ghost_w,
            ghost_e,
            jnp.stack([row_n[0], row_s[0]]),
            jnp.stack([own_w[:rows], own_e[rows : 2 * rows]]),
            row_metric,
            jnp.stack([metric_w, metric_e]),
            stencil_coef,
            norm_gain,
            biases,
            full,
        ),
        smem=1,
        limit=12,
    )
    (out,) = call(
        second_kernel,
        "refine",
        [tile],
        [
            vmem(tile, BF16),
            vmem((2 * DEPTH,) + square, BF16),
            vmem((2,) + square, F32),
            vmem((LANES, 2 * LANES), F32),
            vmem(square, F32),
            vmem((9,) + square, F32),
            vmem((5,) + square, F32),
            vmem((5,) + square, F32),
            vmem((2,) + square, BF16),
            vmem((2, 4 * LANES, 2 * LANES), BF16),
            vmem((2, LANES, BLOCK * LANES), BF16),
            vmem((2, LANES, BLOCK * LANES), BF16),
            vmem((2, LANES, BLOCK * LANES), BF16),
            vmem((BLOCK,) + square, BF16),
            vmem(square, BF16),
            pltpu.SemaphoreType.DMA,
        ],
        (normed, row_t, near_metric, side_metric, lines, sides, stencil_coef, norm_gain, biases, full),
        far_out=True,
    )
    return out


def solution(mesh):
    in_specs = (
        P("lat", "lon", None),
        P(None, "lat", "lon"),
        P(),
        P(),
        P(),
        P(None, ("lat", "lon"), None),
    )
    out_specs = P("lat", "lon", None)
    return jax.shard_map(on_device, mesh=mesh, in_specs=in_specs, out_specs=out_specs, check_vma=False)
```

```python
import functools

import jax
import jax.numpy as jnp
from jax import lax
from jax.experimental import pallas as pl
from jax.experimental.pallas import tpu as pltpu
from jax.sharding import PartitionSpec as P

KMAT = 7
ITERS = 2
EPSILON = 1e-05
LANES = 128
BLOCK = 4
DEPTH = 4 * BLOCK
LINE = 136
ORDER_ONE = (("S", 0), ("T", 0))
ORDER_TWO = (("G", 99), ("M", 99), ("S", 9), ("g", 1), ("S", 9), ("g", 99), ("m", 99), ("O", 9))
F32 = jnp.float32
BF16 = jnp.bfloat16


def twice(a):
    return jnp.concatenate([a, a], axis=1)


def load_vectors(it, coef_ref, gain_ref, bias_ref, rows_s, coef_s, vec_s):
    rows_s[...] = jnp.zeros_like(rows_s)
    rows_s[0:9, :] = coef_ref[:, it, :]
    rows_s[9:10, :] = gain_ref[it : it + 1, :]
    rows_s[10:14, :] = bias_ref[it]
    columns = rows_s[...].T
    for d in range(9):
        coef_s[d] = jnp.broadcast_to(columns[:, d : d + 1], (LANES, LANES))
    for k in range(5):
        factor = 0.5 if k in (2, 3) else 1.0
        vec_s[k] = jnp.broadcast_to(columns[:, 9 + k : 10 + k] * factor, (LANES, LANES))


def load_weights(it, w_ref, m0_s, wg_s):
    def mat(k):
        return w_ref[it, k * LANES : (k + 1) * LANES, :].astype(F32).T

    m0_s[...] = mat(0).astype(BF16)
    h1, h2, h4, h5, h6 = (mat(k) * 0.5 for k in (1, 2, 4, 5, 6))
    parts = [
        jnp.concatenate([h1, h4], 1),
        jnp.concatenate([h2, h5], 1),
        jnp.concatenate([mat(3), h6], 1),
        jnp.concatenate([jnp.zeros_like(h6), h6], 1),
    ]
    for g in range(8):
        for n, part in enumerate(parts):
            wg_s[64 * g + 16 * n : 64 * g + 16 * n + 16, :] = part[16 * g : 16 * g + 16].astype(BF16)


def turned_lines(line):
    wide = line.astype(F32)
    return [wide[1 + b : 129 + b].T for b in range(3)]


def fill_sides(side_s, west, east, side_metric_ref, coef_s, north, south):
    lane = lax.broadcasted_iota(jnp.int32, (LANES, LANES), 1)

    def part(side, column, above, below):
        middle = side.astype(F32).T
        upper, lower = pltpu.roll(middle, 1, 1), pltpu.roll(middle, LANES - 1, 1)
        if above is not None:
            upper = jnp.where(lane == 0, above, upper)
            lower = jnp.where(lane == LANES - 1, below, lower)
        total = None
        for a, cells in enumerate((upper, middle, lower)):
            d = 3 * a + 2 * column
            term = (cells * coef_s[d]) * side_metric_ref[column, d : d + 1, :]
            total = term if total is None else total + term
        return total

    ends = [None] * 4
    if north is not None:
        ends = [north[0][:, 0:1], south[0][:, 0:1], north[2][:, LANES - 1 :], south[2][:, LANES - 1 :]]
    first = part(west, 0, ends[0], ends[1])
    last = pltpu.roll(part(east, 1, ends[2], ends[3]), LANES - 1, 1)
    odd = lane % 2 == 1
    side_s[0] = jnp.where(odd, last, first)
    side_s[1] = jnp.where(odd, first, last)


def stencil_block(g, read_part, metric_ref, side_s, coef_s, vec_s, acc_s, lane, write):
    for pair in range(BLOCK // 2):
        first = g * BLOCK + 2 * pair
        squares = [None, None]
        turns = [lax.rem(2 * LANES - first - r, LANES) for r in range(2)]
        metric = [
            [jnp.broadcast_to(metric_ref[d, pl.ds(first + r, 1), :], (8, LANES)) for r in range(2)]
            for d in range(9)
        ]
        for group in range(LANES // 16):
            rows = [read_part(first - 1 + k, slice(16 * group, 16 * group + 16)).astype(F32) for k in range(4)]
            for half in range(2):
                cs = slice(16 * group + 8 * half, 16 * group + 8 * half + 8)
                cells = [row[8 * half : 8 * half + 8] for row in rows]
                for r in range(2):
                    sums = []
                    for b in range(3):
                        total = None
                        for a in range(3):
                            d = 3 * a + b
                            term = (cells[r + a] * coef_s[d, cs, :]) * metric[d][r]
                            total = term if total is None else total + term
                        sums.append(total)
                    side = pltpu.roll(side_s[r, cs, :], turns[r], 1)
                    west = jnp.where(lane == 0, side, pltpu.roll(sums[0], 1, 1))
                    east = jnp.where(lane == LANES - 1, side, pltpu.roll(sums[2], LANES - 1, 1))
                    total = (sums[1] + west) + east
                    square = total * total
                    squares[r] = square if squares[r] is None else squares[r] + square
                    acc_s[cs, LANES * r : LANES * r + LANES] = total
                yield
        for r in range(2):
            mean = jnp.sum(squares[r], axis=0, keepdims=True) * (1.0 / LANES)
            scale = lax.rsqrt(mean + EPSILON)
            total = acc_s[:, LANES * r : LANES * r + LANES]
            write(2 * pair + r, (total * scale * vec_s[0]).astype(BF16))


def message_block(normed, m0_s, vec_s, write):
    product = jnp.dot(m0_s[...], normed, preferred_element_type=F32)
    yield
    for pair in range(BLOCK // 2):
        ls = slice(2 * LANES * pair, 2 * LANES * (pair + 1))
        write(ls, (product[:, ls] + twice(vec_s[1])).astype(BF16))
        yield


def gates_block(read_message, read_part, wg_s, vec_s, write):
    products = []
    for pair in range(BLOCK // 2):
        ls = slice(2 * LANES * pair, 2 * LANES * (pair + 1))
        whole = slice(0, LANES)
        current = jnp.concatenate([read_part(2 * pair, whole), read_part(2 * pair + 1, whole)], axis=1)
        both = jnp.concatenate([read_message(ls), current], axis=0)
        products.append(jnp.dot(wg_s[...], both, preferred_element_type=F32))
    yield
    for pair in range(BLOCK // 2):
        w = products[pair]
        for g in range(8):
            o = 64 * g
            cs = slice(16 * g, 16 * g + 16)
            old = jnp.concatenate([read_part(2 * pair, cs), read_part(2 * pair + 1, cs)], axis=1).astype(F32)
            update = jnp.tanh(w[o : o + 16] + twice(vec_s[2, cs, :]))
            reset = jnp.tanh(w[o + 16 : o + 32] + twice(vec_s[3, cs, :]))
            inner = (w[o + 32 : o + 48] + twice(vec_s[4, cs, :])) + reset * w[o + 48 : o + 64]
            new = jnp.tanh(inner)
            blend = ((old + new) + update * (old - new)) * 0.5
            blend = blend.astype(BF16)
            for r in range(2):
                write(2 * pair + r, cs, blend[:, LANES * r : LANES * r + LANES])
            yield


def run_stages(stages, order, first, last, guarded):
    names = list(dict.fromkeys(name for name, _ in order))

    def step(s, carry, valid=None):
        here = [name for name in names if valid is None or valid(name)]
        parts = {name: stages[name][0](s - stages[name][1]) for name in here}
        for name, pieces in order:
            for _ in range(pieces if name in here else 0):
                next(parts[name], None)
        for name in here:
            for _ in parts[name]:
                pass
        return carry

    if guarded:
        for s in range(first, last):
            step(s, 0, lambda name: stages[name][2] <= s - stages[name][1] < stages[name][3])
    else:
        lax.fori_loop(first, last, step, 0)


def first_kernel(begin, end, before, wrap, *refs):
    x_ref, metric_ref, side_metric_ref, west_ref, east_ref, coef_ref, gain_ref, bias_ref = refs[:8]
    rest = refs[8:]
    if wrap:
        north_ref, south_ref = rest[:2]
        rest = rest[2:]
    if before:
        old_row_ref, old_normed_ref = rest[:2]
        rest = rest[2:]
    row_ref, normed_ref, side_s, acc_s, rows_s, coef_s, vec_s = rest
    lane = lax.broadcasted_iota(jnp.int32, (8, LANES), 1)
    count = x_ref.shape[0] // BLOCK
    load_vectors(0, coef_ref, gain_ref, bias_ref, rows_s, coef_s, vec_s)
    north = south = None
    if wrap:
        north, south = turned_lines(north_ref[...]), turned_lines(south_ref[...])
        row_ref[BLOCK - 1] = north[1].astype(BF16)
        row_ref[(count + 1) * BLOCK] = south[1].astype(BF16)
    fill_sides(side_s, west_ref[...], east_ref[...], side_metric_ref, coef_s, north, south)

    def turn(g):
        for r in range(BLOCK):
            row = x_ref[g * BLOCK + r].T
            yield
            row_ref[(g + 1) * BLOCK + r] = row
            yield

    def stencil(g):
        def write(r, normed):
            normed_ref[g * BLOCK + r] = normed

        yield from stencil_block(
            g, lambda q, cs: row_ref[q + BLOCK, cs, :], metric_ref, side_s, coef_s, vec_s, acc_s, lane, write
        )

    def copy(g, carry):
        for r in range(BLOCK):
            row_ref[(g + 1) * BLOCK + r] = old_row_ref[(g + 1) * BLOCK + r]
            normed_ref[g * BLOCK + r] = old_normed_ref[g * BLOCK + r]
        return carry

    def span(lo, hi):
        low, high = max(lo - 1, 0), min(hi + 1, count)
        stages = {"T": (turn, 0, low, high), "S": (stencil, 2, lo, hi)}
        run_stages(stages, (("T", 0),), low, lo + 2, True)
        full = min(high, hi + 2)
        run_stages(stages, ORDER_ONE, lo + 2, full, False)
        run_stages(stages, (("S", 0),), full, hi + 2, True)

    if before:
        lax.fori_loop(1, 1 + before, copy, 0)
    if wrap:
        span(0, 1)
    span(begin, end)


def second_kernel(normed_ref, row_ref, metric_ref, side_metric_ref, lines_ref, sides_ref, coef_ref, gain_ref, bias_ref, w_ref,
                  out_hbm, out_ref, state_s, side_s, acc_s, rows_s, coef_s, vec_s, old_vec_s, m0_s, wg_s,
                  msg1_s, msg2_s, normed_s, flip_s, south_s, sem):
    count = out_ref.shape[0] // BLOCK
    lane = lax.broadcasted_iota(jnp.int32, (8, LANES), 1)
    load_vectors(0, coef_ref, gain_ref, bias_ref, rows_s, coef_s, old_vec_s)
    load_vectors(1, coef_ref, gain_ref, bias_ref, rows_s, coef_s, vec_s)
    for it in range(2):
        load_weights(it, w_ref, m0_s.at[it], wg_s.at[it])
    north, south = turned_lines(lines_ref[0]), turned_lines(lines_ref[1])
    state_s[2 * DEPTH - 1] = north[1].astype(BF16)
    south_s[...] = south[1].astype(BF16)
    fill_sides(side_s, sides_ref[0], sides_ref[1], side_metric_ref, coef_s, north, south)

    def message_one(g):
        buf = lax.rem(g, 2)
        normed = jnp.concatenate([normed_ref[g * BLOCK + r] for r in range(BLOCK)], axis=1)

        def write(ls, value):
            msg1_s[buf, :, ls] = value

        yield from message_block(normed, m0_s.at[0], old_vec_s, write)

    def gates_one(g):
        buf = lax.rem(g, 2)

        def write(r, cs, value):
            state_s[lax.rem(g * BLOCK + r, 2 * DEPTH), cs, :] = value

        yield from gates_block(lambda ls: msg1_s[buf, :, ls], lambda r, cs: row_ref[(g + 1) * BLOCK + r, cs, :], wg_s.at[0], old_vec_s, write)

    def stencil(g):
        buf = lax.rem(g, 2)

        def write(r, normed):
            normed_s[buf, :, LANES * r : LANES * r + LANES] = normed

        def part(q, cs):
            return state_s[lax.rem(q + 2 * DEPTH, 2 * DEPTH), cs, :]

        yield from stencil_block(g, part, metric_ref, side_s, coef_s, vec_s, acc_s, lane, write)

    def message_two(g):
        buf = lax.rem(g, 2)

        def write(ls, value):
            msg2_s[buf, :, ls] = value

        yield from message_block(normed_s[buf], m0_s.at[1], vec_s, write)

    def gates_two(g):
        buf = lax.rem(g, 2)

        def write(r, cs, value):
            flip_s[r, cs, :] = value

        yield from gates_block(
            lambda ls: msg2_s[buf, :, ls],
            lambda r, cs: state_s[lax.rem(g * BLOCK + r, 2 * DEPTH), cs, :],
            wg_s.at[1],
            vec_s,
            write,
        )
        for r in range(BLOCK):
            out_ref[g * BLOCK + r] = flip_s[r].T

    def store(g):
        at = pl.ds(g * BLOCK, BLOCK)
        pltpu.make_async_copy(out_ref.at[at], out_hbm.at[at], sem).start()
        yield

    stages = {
        "m": (message_one, 0, 0, count),
        "g": (gates_one, 1, 0, count),
        "S": (stencil, 3, 0, count),
        "M": (message_two, 4, 0, count),
        "G": (gates_two, 5, 0, count),
        "O": (store, 5, 0, count),
    }
    run_stages(stages, ORDER_TWO, 0, 5, True)
    run_stages(stages, ORDER_TWO, 5, count, False)
    state_s[(count * BLOCK) % (2 * DEPTH)] = south_s[...]
    run_stages(stages, ORDER_TWO, count, count + 5, True)
    pltpu.make_async_copy(out_ref, out_hbm, sem).wait()


def fetch_kernel(state_hbm, metric_hbm, state_ref, metric_ref, sems):
    part = state_ref.shape[0] // 8
    copies = [pltpu.make_async_copy(metric_hbm, metric_ref, sems.at[8])]
    for n in range(8):
        at = pl.ds(n * part, part)
        copies.append(pltpu.make_async_copy(state_hbm.at[at], state_ref.at[at], sems.at[n]))
    for copy in copies:
        copy.start()
    for copy in copies:
        copy.wait()
    for a in range(3):
        metric_ref[3 * a] = pltpu.roll(metric_ref[3 * a], LANES - 1, 1)
        metric_ref[3 * a + 2] = pltpu.roll(metric_ref[3 * a + 2], 1, 1)


def edge_kernel(flags_ref, state_hbm, metric_hbm, near_ref, far_ref, rows_ref, sides_ref, west_s, east_s, metric_ref,
                strip_s, line_s, sems):
    rows, cols = state_hbm.shape[0], state_hbm.shape[1]
    copies = [
        pltpu.make_async_copy(state_hbm.at[:, 0:16, :], west_s, sems.at[0]),
        pltpu.make_async_copy(state_hbm.at[:, cols - 16 : cols, :], east_s, sems.at[1]),
        pltpu.make_async_copy(metric_hbm, metric_ref, sems.at[2]),
    ]
    for copy in copies:
        copy.start()
    for copy in copies:
        copy.wait()
    east_near = flags_ref[0] == 1
    out = lax.broadcasted_iota(jnp.int32, (32, 256), 0)
    source = lax.broadcasted_iota(jnp.int32, (32, 256), 1)

    def picker(first):
        return jnp.where(source == (out % 16) * 16 + first + out // 16, 1.0, 0.0).astype(BF16)

    pick_w, pick_e = picker(0), picker(14)
    for part in range(rows // 16):
        at = slice(16 * part, 16 * part + 16)
        west = west_s[at].reshape(256, LANES)
        east = east_s[at].reshape(256, LANES)
        west = jnp.dot(pick_w, west, preferred_element_type=F32)
        east = jnp.dot(pick_e, east, preferred_element_type=F32)
        near = jnp.where(east_near, east, west).astype(BF16)
        far = jnp.where(east_near, west, east).astype(BF16)
        for n in range(2):
            to = n * rows + 16 * part
            near_ref[to : to + 16, :] = near[16 * n : 16 * n + 16]
            far_ref[to : to + 16, :] = far[16 * n : 16 * n + 16]
    line_s[...] = jnp.zeros_like(line_s)
    for d in range(9):
        upright = metric_ref[d].T
        line_s[0, d : d + 1, :] = upright[0:1]
        line_s[1, d : d + 1, :] = upright[LANES - 1 : LANES]
        line_s[2, d : d + 1, :] = metric_ref[d, 0:1, :]
        line_s[3, d : d + 1, :] = metric_ref[d, rows - 1 : rows, :]
    for n in range(4):
        high = line_s[n].astype(BF16)
        strip_s[n, 0:16, :] = high
        strip_s[n, 16:32, :] = (line_s[n] - high.astype(F32)).astype(BF16)
    west, east = strip_s[0].astype(F32), strip_s[1].astype(F32)
    near_ref[2 * rows : 2 * rows + 32, :] = jnp.where(east_near, east, west).astype(BF16)
    far_ref[2 * rows : 2 * rows + 32, :] = jnp.where(east_near, west, east).astype(BF16)
    sides_ref[...] = line_s[0:2]
    rows_ref[0] = strip_s[2]
    rows_ref[1] = strip_s[3]


def ring_kernel(flags_ref, north_ref, south_ref, west_ref, east_ref, own_rows_ref, own_cols_ref,
                row_metric_ref, col_metric_ref, coef_ref, gain_ref, bias_ref, w_ref,
                lines_ref, sides_ref, line_s, metric_s, new_s):
    polar = [flags_ref[1] == 1, flags_ref[2] == 1]
    ghost = [north_ref, south_ref]
    side = [west_ref, east_ref]

    def put(strip, n, value):
        line_s[strip, n, 8 : 8 + LINE, :] = value

    for e in range(2):
        outer = ghost[e][1].astype(F32)
        inner = own_rows_ref[e].astype(F32)
        before, after = (outer, inner) if e == 0 else (inner, outer)
        put(e, 0, jnp.where(polar[e], after, before))
        put(e, 1, ghost[e][0].astype(F32))
        put(e, 2, jnp.where(polar[e], before, after))
    for e in range(2):
        columns = [side[e][0], side[e][1], own_cols_ref[e]] if e == 0 else [side[e][1], side[e][0], own_cols_ref[e]]
        if e == 1:
            columns = columns[::-1]
        for n in range(3):
            at = n if e == 0 else 129 + n
            line_s[2 + e, n, 0:8, :] = jnp.zeros((8, LANES), F32)
            line_s[2 + e, n, 136:152, :] = jnp.zeros((16, LANES), F32)
            line_s[2 + e, n, 10:138, :] = columns[n].astype(F32)
            line_s[2 + e, n, 9:10, :] = line_s[0, 1, 8 + at : 9 + at, :]
            line_s[2 + e, n, 138:139, :] = line_s[1, 1, 8 + at : 9 + at, :]

    def upright(packed):
        both = packed.astype(F32)
        tall = jnp.concatenate([both[0:16] + both[16:32], jnp.zeros((LANES - 16, LANES), F32)], axis=0)
        return tall.T

    metric_s[...] = jnp.zeros_like(metric_s)
    for e in range(2):
        metric_s[e, 2:130, :] = upright(row_metric_ref[e, 0:32])
        ends = upright(row_metric_ref[e, 32:64])
        metric_s[e, 1:2, :] = ends[0:1]
        metric_s[e, 130:131, :] = ends[1:2]
        metric_s[2 + e, 2:130, :] = upright(col_metric_ref[e])
    normed = []
    old = []
    for strip in range(4):
        metric = metric_s[strip]
        total = None
        for n in range(3):
            for shift in range(3):
                d = 3 * n + shift if strip < 2 else 3 * shift + n
                cells = line_s[strip, n, 7 + shift : 7 + shift + LINE, :]
                term = metric[:, d : d + 1] * coef_ref[d, 0:1, :] * cells
                total = term if total is None else total + term
        scale = lax.rsqrt(jnp.mean(total * total, axis=1, keepdims=True) + EPSILON)
        normed.append(total * scale * gain_ref[0:1, :])
        old.append(line_s[strip, 1, 8 : 8 + LINE, :])
    normed = jnp.concatenate(normed, 0).astype(BF16)
    old = jnp.concatenate(old, 0)

    def mat(k):
        return w_ref[0, k * LANES : (k + 1) * LANES, :]

    def dot(a, k):
        return jnp.dot(a, mat(k), preferred_element_type=F32)

    message = (dot(normed, 0) + bias_ref[0, 0:1, :]).astype(BF16)
    hidden = old.astype(BF16)
    update = 0.5 * jnp.tanh(0.5 * (dot(message, 1) + dot(hidden, 4) + bias_ref[0, 1:2, :])) + 0.5
    reset = 0.5 * jnp.tanh(0.5 * (dot(message, 2) + dot(hidden, 5) + bias_ref[0, 2:3, :])) + 0.5
    new = jnp.tanh(dot(message, 3) + bias_ref[0, 3:4, :] + reset * dot(hidden, 6))
    new_s[...] = (1.0 - update) * new + update * old
    for e in range(2):
        lines_ref[e] = new_s[e * LINE : (e + 1) * LINE, :].astype(BF16)
        sides_ref[e] = new_s[(2 + e) * LINE + 2 : (2 + e) * LINE + 130, :].astype(BF16)


def call(kernel, name, outs, scratch, args, smem=0, hbm=0, far_out=False, flops=0, traffic=0, limit=24):
    vmem = pl.BlockSpec(memory_space=pltpu.VMEM)
    scalar = pl.BlockSpec(memory_space=pltpu.SMEM)
    far = pl.BlockSpec(memory_space=pltpu.HBM)
    return pl.pallas_call(
        kernel,
        in_specs=[scalar] * smem + [far] * hbm + [vmem] * (len(args) - smem - hbm),
        out_specs=[far if far_out else vmem] * len(outs),
        out_shape=[s if hasattr(s, "dtype") else jax.ShapeDtypeStruct(s, BF16) for s in outs],
        scratch_shapes=scratch,
        compiler_params=pltpu.CompilerParams(vmem_limit_bytes=limit * 1024 * 1024),
        cost_estimate=pl.CostEstimate(flops=flops, bytes_accessed=traffic, transcendentals=0),
        name=name,
    )(*args)


def swap(mesh_shape, partner, value):
    lat, lon = mesh_shape
    pairs = [(i * lon + k, partner(i, k)[0] * lon + partner(i, k)[1]) for i in range(lat) for k in range(lon)]
    return lax.ppermute(value, ("lat", "lon"), pairs)


def on_device(state, edge_metric, stencil_coef, norm_gain, biases, weights):
    lat, lon = lax.axis_size("lat"), lax.axis_size("lon")
    shape = (lat, lon)
    half = lon // 2
    i, k = lax.axis_index("lat"), lax.axis_index("lon")
    rows, cols, channels = state.shape
    k_even = k % 2 == 0
    i_even = i % 2 == 0

    def ordered(first, mine, theirs):
        return jnp.where(first, jnp.concatenate([mine, theirs]), jnp.concatenate([theirs, mine]))

    def halves(first, a, b):
        return jnp.where(first, a, b), jnp.where(first, b, a)

    def after(value, *others):
        return lax.optimization_barrier((value,) + others)[0]

    shard = weights.transpose(1, 0, 2).reshape(-1, channels)
    stencil_coef = stencil_coef.transpose(1, 0, 2)

    vmem = pltpu.VMEM
    flags = jnp.stack([k_even, i == 0, i == lat - 1]).astype(jnp.int32)
    size = 2 * rows + 32
    near, far, row_metrics, side_metric = call(
        edge_kernel,
        "edges",
        [(size, channels), (size, channels), (2, 32, cols), jax.ShapeDtypeStruct((2, 16, rows), F32)],
        [
            vmem((rows, 16, channels), BF16),
            vmem((rows, 16, channels), BF16),
            vmem(edge_metric.shape, F32),
            vmem((4, 32, LANES), BF16),
            vmem((4, 16, LANES), F32),
            pltpu.SemaphoreType.DMA((3,)),
        ],
        (flags, state, edge_metric),
        smem=1,
        hbm=2,
        limit=12,
    )
    got_near = swap(shape, lambda i, k: (i, k ^ 1), jnp.concatenate([near, shard]))
    size = 2 * rows + 32
    shard = ordered(k_even, shard, got_near[size:])
    far_shard = jnp.concatenate([far, shard])
    got_far = swap(shape, lambda i, k: (i, (k + 1) % lon if k % 2 else (k - 1) % lon), far_shard)
    near_state, near_metric = call(
        fetch_kernel,
        "fetch",
        [state, edge_metric],
        [pltpu.SemaphoreType.DMA((9,))],
        (after(state, far_shard), edge_metric),
        hbm=2,
        traffic=8 * state.size,
        limit=12,
    )
    shard = ordered(jnp.logical_not(k_even), shard, got_far[size:])
    in_e, in_w = halves(k_even, got_near[:size], got_far[:size])
    ghost_w, ghost_e = (a[: 2 * rows].reshape(2, rows, channels) for a in (in_w, in_e))
    metric_w, metric_e = in_w[2 * rows :], in_e[2 * rows :]
    own_e, own_w = halves(k_even, near, far)

    def extended(row, inner):
        lines = []
        for q in (row, inner):
            fill = jnp.zeros((LINE - cols - 4, channels), BF16)
            lines.append(jnp.concatenate([ghost_w[:, q], near_state[q], ghost_e[:, q], fill]))
        return jnp.stack(lines)

    def extended_metric(row, body):
        ends = jnp.concatenate([metric_w[:, row : row + 1], metric_e[:, row : row + 1]], axis=1)
        ends = jnp.pad(ends, ((0, 0), (0, LANES - 2)))
        return jnp.concatenate([body, ends])

    row_n, row_s = extended(0, 1), extended(rows - 1, rows - 2)
    out_n = jnp.concatenate([row_n.reshape(-1, channels), extended_metric(0, row_metrics[0])])
    out_s = jnp.concatenate([row_s.reshape(-1, channels), extended_metric(rows - 1, row_metrics[1])])
    size = out_n.shape[0]
    send_a, send_b = halves(i_even, out_s, out_n)
    send_a = jnp.concatenate([send_a, shard])

    def across(i, k):
        if i == 0 or i == lat - 1:
            return i, (k + half) % lon
        return (i + 1, k) if i % 2 else (i - 1, k)

    got_a = swap(shape, lambda i, k: (i ^ 1, k), send_a)
    got_b = swap(shape, across, send_b)

    tile = state.shape
    square = (LANES, LANES)
    count = rows // BLOCK
    cuts = [1, 1 + (count - 1) // 3, 1 + 2 * (count - 1) // 3, count]

    def aggregate(part, side_w, more):
        begin, end = cuts[part], cuts[part + 1]
        return call(
            functools.partial(first_kernel, begin, end, begin - 1, part == 2),
            "aggregate%d" % part,
            [(rows + 2 * BLOCK,) + square, tile],
            [
                vmem((2,) + square, F32),
                vmem((LANES, 2 * LANES), F32),
                vmem(square, F32),
                vmem((9,) + square, F32),
                vmem((5,) + square, F32),
            ],
            (near_state, near_metric, side_metric, side_w, ghost_e[0], stencil_coef, norm_gain, biases) + more,
            flops=20 * state.size,
            traffic=8 * state.size,
        )

    held = aggregate(0, after(ghost_w[1], send_a, send_b), ())

    shard = ordered((i & 1) == 0, shard, got_a[size:])
    in_s, in_n = halves(i_even, got_a[:size], got_b)
    ghost_n, ghost_s = (a[: 2 * LINE].reshape(2, LINE, channels) for a in (in_n, in_s))
    row_metric = jnp.stack([in_n[2 * LINE :], in_s[2 * LINE :]])

    shard = shard.reshape(2, 4, -1, channels)
    bit = 4
    while bit < lon:
        mine = after(shard, *held) if bit == 4 else shard
        got = swap(shape, lambda i, k, bit=bit: (i, k ^ bit), mine)
        low = (k & bit) == 0
        shard = jnp.where(
            low, jnp.concatenate([shard, got], axis=1), jnp.concatenate([got, shard], axis=1)
        )
        if bit == 4:
            held = aggregate(1, after(ghost_w[1], mine), tuple(held))
        bit *= 2
    place = k % 4
    shard = jnp.where(
        place == 0,
        jnp.roll(shard, -2, axis=1),
        jnp.where(place == 3, jnp.roll(shard, 2, axis=1), shard),
    )
    shard = shard.reshape(-1, channels)
    bit = 2
    while bit < lat:
        mine = after(shard, *held) if bit == 2 else shard
        got = swap(shape, lambda i, k, bit=bit: (i ^ bit, k), mine)
        shard = ordered((i & bit) == 0, shard, got)
        if bit == 2:
            held = aggregate(2, after(ghost_w[1], mine), (ghost_n[0], ghost_s[0]) + tuple(held))
        bit *= 2
    row_t, normed = held
    full = shard.reshape(-1, ITERS, channels).transpose(1, 0, 2)

    lines, sides = call(
        ring_kernel,
        "border",
        [(2, LINE, channels), (2, rows, channels)],
        [vmem((4, 3, LINE + 16, LANES), F32), vmem((4, LINE, LANES), F32), vmem((4 * LINE, LANES), F32)],
        (
            flags,
            ghost_n,
            ghost_s,
            ghost_w,
            ghost_e,
            jnp.stack([row_n[0], row_s[0]]),
            jnp.stack([own_w[:rows], own_e[rows : 2 * rows]]),
            row_metric,
            jnp.stack([metric_w, metric_e]),
            stencil_coef,
            norm_gain,
            biases,
            full,
        ),
        smem=1,
        limit=12,
    )
    (out,) = call(
        second_kernel,
        "refine",
        [tile],
        [
            vmem(tile, BF16),
            vmem((2 * DEPTH,) + square, BF16),
            vmem((2,) + square, F32),
            vmem((LANES, 2 * LANES), F32),
            vmem(square, F32),
            vmem((9,) + square, F32),
            vmem((5,) + square, F32),
            vmem((5,) + square, F32),
            vmem((2,) + square, BF16),
            vmem((2, 4 * LANES, 2 * LANES), BF16),
            vmem((2, LANES, BLOCK * LANES), BF16),
            vmem((2, LANES, BLOCK * LANES), BF16),
            vmem((2, LANES, BLOCK * LANES), BF16),
            vmem((BLOCK,) + square, BF16),
            vmem(square, BF16),
            pltpu.SemaphoreType.DMA,
        ],
        (normed, row_t, near_metric, side_metric, lines, sides, stencil_coef, norm_gain, biases, full),
        far_out=True,
    )
    return out


def solution(mesh):
    in_specs = (
        P("lat", "lon", None),
        P(None, "lat", "lon"),
        P(),
        P(),
        P(),
        P(None, ("lat", "lon"), None),
    )
    out_specs = P("lat", "lon", None)
    return jax.shard_map(on_device, mesh=mesh, in_specs=in_specs, out_specs=out_specs, check_vma=False)
```
